32 devices in a mesh: groups: 2 (over y), dom: 4 (over z), batch: 2 (over x), sub: 2 (over core).
Axes of the slice: x: 2, y: 2, z: 4, core: 2. Of those that a mesh axis runs over, the one named last changes fastest.
Arguments:
- solution: float32 [32768], P(('groups', 'dom', 'batch', 'sub')), parts along dimension 0, may hold values from -6 to 6
- residual: float32 [32768], P(('groups', 'dom', 'batch', 'sub')), parts along dimension 0, may hold values from -18 to 18
- direction: float32 [32768], P(('groups', 'dom', 'batch', 'sub')), parts along dimension 0, may hold values from -18 to 18
- inverse_diagonal: float32 [32768], P(('groups', 'dom', 'batch', 'sub')), parts along dimension 0, may hold values from 0.25 to 2
- schur_blocks: float32 [96, 602, 602], P(('groups', 'dom', 'batch', 'sub')), parts along dimension 0, may hold values from -1 to 4, as said below
- elem_dofs: int32 [96, 602], P(('groups', 'dom', 'batch', 'sub')), parts along dimension 0, may hold values from 0 to 4095, as said below
- element_order: int32 [96], P(('groups', 'dom', 'batch', 'sub')), parts along dimension 0, may hold values from 4 to 10
- left_slots: int32 [32, 256], P(('groups', 'dom', 'batch', 'sub')), parts along dimension 0, may hold values from 0 to 1023, as said below
- right_slots: int32 [32, 256], P(('groups', 'dom', 'batch', 'sub')), parts along dimension 0, may hold values from 0 to 1023, as said below
- share_count: int32 [32, 2], P(('groups', 'dom', 'batch', 'sub')), parts along dimension 0, may hold values from 0 to 256, as said below
Outputs:
- new_solution: float32 [32768], P(('groups', 'dom', 'batch', 'sub')), parts along dimension 0
- new_residual: float32 [32768], P(('groups', 'dom', 'batch', 'sub')), parts along dimension 0
- new_direction: float32 [32768], P(('groups', 'dom', 'batch', 'sub')), parts along dimension 0
The draws below stay inside these ranges and needn't reach their ends.
There are 2 independent parts, one for each index of `groups`. The reference program is written for one: setup_inputs(seed, part) draws one part's arguments, and reference() takes and returns one part's arrays. A program takes and returns all parts, laid end to end along the dimension named above; each array names one. Nothing has to cross between parts.
Inputs may be any that keep to these rules, and one draw needn't show every extreme that they name: The slots of left_slots[c] and right_slots[c] are all distinct. `right_slots`: distinct from left_slots of the same piece and among themselves. share_count[c, 1] equals share_count[c + 4, 0]; the first partition's left counts and the last partition's right counts are 0; 256 is reached in every draw. `elem_dofs`: every slot named by an element of piece c lies in piece c, or in the piece just before or just after it within the same partition, counted cyclically over the partition's 2 * 2 pieces. `schur_blocks`: symmetric positive definite blocks.
All inputs are finite; a program needn't handle non-finite values.
Results may differ from the reference program's by a relative error of at most 0.000064.
Values sent between devices are 32-bit elements; how exact they have to be, the bound alone decides.
No kernel may reach another device: no remote copies, remote signals or barrier semaphores. Data moves between devices by JAX's collectives and lax.ppermute only.
A program may use at most 64 MiB of HBM per device.

```python
import math
import jax
import jax.numpy as jnp
from jax import lax

NB = 602
ORDER = 10
E_DEV = 3
LDP = 1024
SH = 256
LOCAL = 4096
PIECES = 16
ELEMS = 48
NDOF = 16384
N_BATCH = 2
N_SUB = 2


def slot_lists(key):
    keys = jax.random.split(key, PIECES)
    shuffled = jax.vmap(lambda one_key: jax.random.permutation(one_key, LDP))(keys)
    return (shuffled[:, :SH].astype(jnp.int32), shuffled[:, SH:2 * SH].astype(jnp.int32))


def rising_scale():
    position = jnp.arange(NDOF, dtype=jnp.float32) / NDOF
    return 1.0 + 2.0 * position


def draw_left_slots(key, part):
    first_list, second_list = slot_lists(key)
    return first_list


def draw_right_slots(key, part):
    first_list, second_list = slot_lists(key)
    return second_list


def draw_elem_dofs(key, part):
    key = jax.random.fold_in(key, 14)
    side_key, slot_key = jax.random.split(key)
    group_size = N_BATCH * N_SUB
    piece_in_group = jnp.arange(ELEMS, dtype=jnp.int32) // E_DEV % group_size
    pick = jax.random.randint(side_key, (ELEMS, NB), 0, 10)
    offset = jnp.where(pick == 0, -1, jnp.where(pick == 1, 1, 0)).astype(jnp.int32)
    target = (piece_in_group[:, None] + offset + group_size) % group_size
    slot = jax.random.randint(slot_key, (ELEMS, NB), 0, LDP)
    return (target * LDP + slot).astype(jnp.int32)


def draw_residual(key, part):
    key = jax.random.fold_in(key, 11)
    values = jnp.clip(jax.random.normal(key, (NDOF,), jnp.float32), -6.0, 6.0)
    return values * rising_scale()


def draw_direction(key, part):
    key = jax.random.fold_in(key, 12)
    values = jnp.clip(jax.random.normal(key, (NDOF,), jnp.float32), -6.0, 6.0)
    return values * rising_scale()


def draw_share_count(key, part):
    key = jax.random.fold_in(key, 13)
    first_key, second_key = jax.random.split(key)
    group_size = N_BATCH * N_SUB
    pair_total = PIECES - group_size
    counts = jax.random.randint(first_key, (pair_total,), SH // 2, SH + 1)
    chosen = jax.random.randint(second_key, (), 0, pair_total)
    counts = jnp.where(jnp.arange(pair_total) == chosen, SH, counts).astype(jnp.int32)
    padding = jnp.zeros((group_size,), jnp.int32)
    return jnp.stack([jnp.concatenate([padding, counts]), jnp.concatenate([counts, padding])], axis=1)


def draw_schur_blocks(key, part):
    key = jax.random.fold_in(key, 7)
    noise_key, diag_key = jax.random.split(key)
    noise = jnp.clip(jax.random.normal(noise_key, (ELEMS, NB, NB), jnp.float32), -6.0, 6.0) * 0.35
    noise = noise / jnp.sqrt(jnp.float32(NB))
    diagonal = jax.random.uniform(diag_key, (ELEMS, NB), jnp.float32, 1.6, 3.0)
    return noise + jnp.swapaxes(noise, 1, 2) + jnp.eye(NB, dtype=jnp.float32)[None] * diagonal[:, :, None]


def touch_ends(array, rng, smallest, high):
    spot = [jax.random.randint(jax.random.fold_in(rng, axis), (), 0, length) for axis, length in enumerate(array.shape)]
    widest = array.shape.index(max(array.shape))
    neighbour = spot[:widest] + [(spot[widest] + 1) % array.shape[widest]] + spot[widest + 1:]
    return array.at[tuple(spot)].set(smallest).at[tuple(neighbour)].set(high)


def shard_levels(rng, dims, cuts, smallest, largest):
    def one(dim, parts):
        draws = jax.random.uniform(jax.random.fold_in(jax.random.fold_in(rng, 6), dim), (parts,), jnp.float32, smallest / len(cuts), largest / len(cuts))
        return jnp.repeat(jnp.exp(draws), dims[dim] // parts).reshape((-1,) + (1,) * (len(dims) - dim - 1))

    gain = one(*cuts[0])
    for cut in cuts[1:]:
        gain = gain * one(*cut)
    return gain


def centred(stream_key, extent, spread, bound, cuts=(), kind=jnp.bfloat16):
    result = jax.random.normal(stream_key, extent, jnp.float32) * spread
    if len(cuts) > 0:
        result = shard_levels(stream_key, extent, cuts, -0.22, 0.18) * result
    return jnp.clip(result, min=-bound, max=bound).astype(kind)


def setup_inputs(seed: int = 0, part: int = 0) -> dict:
    arg_keys = jax.random.split(jax.random.key(seed), 11)
    part_keys = jax.random.split(jax.random.fold_in(arg_keys[10], part), 11)
    solution = centred(part_keys[0], (NDOF,), 1.0, 6.0, ((0, 16),), jnp.float32)
    residual = draw_residual(jax.random.fold_in(jax.random.fold_in(arg_keys[10], part), 71), part)
    direction = draw_direction(jax.random.fold_in(jax.random.fold_in(arg_keys[10], part), 71), part)
    inverse_diagonal = jnp.clip(jnp.exp(math.log(2.0) - 2.0794415 * jax.random.uniform(part_keys[3], (NDOF,), jnp.float32) ** shard_levels(part_keys[3], (NDOF,), ((0, 16),), -0.2, 0.2)), 0.25, 2.0)
    schur_blocks = draw_schur_blocks(jax.random.fold_in(jax.random.fold_in(arg_keys[10], part), 71), part)
    elem_dofs = draw_elem_dofs(jax.random.fold_in(jax.random.fold_in(arg_keys[10], part), 71), part)
    element_order = touch_ends(jax.random.randint(part_keys[6], (ELEMS,), 4, ORDER + 1), jax.random.fold_in(part_keys[6], 1), 4, ORDER).astype(jnp.int32)
    left_slots = draw_left_slots(jax.random.fold_in(jax.random.fold_in(arg_keys[10], part), 71), part)
    right_slots = draw_right_slots(jax.random.fold_in(jax.random.fold_in(arg_keys[10], part), 71), part)
    share_count = draw_share_count(jax.random.fold_in(jax.random.fold_in(arg_keys[10], part), 71), part)
    return {"solution": solution, "residual": residual, "direction": direction, "inverse_diagonal": inverse_diagonal, "schur_blocks": schur_blocks, "elem_dofs": elem_dofs, "element_order": element_order, "left_slots": left_slots, "right_slots": right_slots, "share_count": share_count}


def reference(solution, residual, direction, inverse_diagonal, schur_blocks, elem_dofs, element_order, left_slots, right_slots, share_count):
    group_size = N_BATCH * N_SUB
    partition = jnp.arange(ELEMS, dtype=jnp.int32) // (E_DEV * group_size)
    global_dofs = (elem_dofs + (partition * LOCAL)[:, None]).astype(jnp.int32)
    live_count = (NB * (6 * element_order * element_order + 2)) // (6 * ORDER * ORDER + 2)
    active = jnp.arange(NB, dtype=jnp.int32)[None, :] < live_count[:, None]
    element_in = jnp.where(active, direction[global_dofs], 0.0)
    element_out = jnp.einsum("eij,ej->ei", schur_blocks, element_in, precision=lax.Precision.HIGHEST)
    element_out = jnp.where(active, element_out, 0.0)
    partial_sum = jnp.zeros((NDOF,), jnp.float32).at[global_dofs.reshape(-1)].add(element_out.reshape(-1))
    base = (jnp.arange(PIECES, dtype=jnp.int32) * LDP)[:, None]
    left_global = (left_slots + base).astype(jnp.int32)
    right_global = (right_slots + base).astype(jnp.int32)
    pair_index = jnp.arange(SH, dtype=jnp.int32)[None, :]
    left_active = pair_index < share_count[:, 0:1]
    pair_active = pair_index < share_count[:-group_size, 1:2]
    sender = right_global[:-group_size]
    receiver = left_global[group_size:]
    applied = partial_sum.at[receiver.reshape(-1)].add(jnp.where(pair_active, partial_sum[sender], 0.0).reshape(-1))
    applied = applied.at[sender.reshape(-1)].add(jnp.where(pair_active, partial_sum[receiver], 0.0).reshape(-1))
    owner_mask = jnp.ones((NDOF,), jnp.float32).at[left_global.reshape(-1)].set(jnp.where(left_active, 0.0, 1.0).reshape(-1))
    old_norm = jnp.sum(owner_mask * residual * inverse_diagonal * residual)
    curvature = jnp.sum(owner_mask * direction * applied)
    step_size = old_norm / curvature
    new_solution = solution + step_size * direction
    new_residual = residual - step_size * applied
    precond = inverse_diagonal * new_residual
    new_norm = jnp.sum(owner_mask * new_residual * precond)
    new_direction = precond + (new_norm / old_norm) * direction
    return new_solution, new_residual, new_direction
```

```python
import jax
import jax.numpy as jnp
from jax import lax
from jax.sharding import PartitionSpec as P

ORDER = 10


def padded(array, sides, width):
    for axis, dim in sides:
        count, length = (lax.axis_size(axis), array.shape[dim])
        up = [(i, (i + 1) % count) for i in range(count)]
        down = [(j, i) for i, j in up]
        last = lax.slice_in_dim(array, length - width, length, axis=dim)
        initial = lax.slice_in_dim(array, 0, width, axis=dim)
        before = lax.ppermute(last, axis, up)
        after = lax.ppermute(initial, axis, down)
        array = jnp.concatenate([before, array, after], axis=dim)
    return array


def shifted(block, axis, distance):
    devices = range(lax.axis_size(axis))
    route = [((i - distance) % len(devices), i) for i in devices]
    return lax.ppermute(block, axis, route)


def passed_along(value, axis, steps):
    count = lax.axis_size(axis)
    initial, last = (max(0, -steps), min(count, count - steps))
    return lax.ppermute(value, axis, [(source, source + steps) for source in range(initial, last)])


def summed(value, axes):
    for axis in axes:
        count, distance = (lax.axis_size(axis), 1)
        if count & (count - 1):
            value = lax.psum(value, axis)
            continue
        while distance < count:
            swap = [(i, i ^ distance) for i in range(count)]
            value = value + lax.ppermute(value, axis, swap)
            distance *= 2
    return value


def local(
    solution,
    residual,
    direction,
    inverse_diagonal,
    schur_blocks,
    elem_dofs,
    element_order,
    left_slots,
    right_slots,
    share_count,
):
    piece_len = residual.shape[0]
    block_size = schur_blocks.shape[1]
    group_count = lax.axis_size(("batch", "sub"))
    local_len = piece_len * group_count
    live_count = block_size * (6 * element_order * element_order + 2) // (6 * ORDER * ORDER + 2)
    active = jnp.arange(block_size, dtype=jnp.int32)[None, :] < live_count[:, None]
    my_index = lax.axis_index(("batch", "sub"))
    window_start = (my_index + group_count - 1) % group_count * piece_len
    relative = (elem_dofs - window_start + local_len) % local_len
    window = padded(direction, ((("batch", "sub"), 0),), piece_len)
    element_in = jnp.take(window, relative, axis=0)
    element_in = jnp.where(active, element_in, 0.0)
    element_out = jnp.einsum(
        "eij,ej->ei", schur_blocks, element_in, precision=lax.Precision.HIGHEST
    )
    element_out = jnp.where(active, element_out, 0.0)
    window_sum = (
        jnp.zeros((3 * piece_len,), jnp.float32)
        .at[relative.reshape(-1)]
        .add(element_out.reshape(-1))
    )
    from_next = shifted(window_sum[:piece_len], ("batch", "sub"), -1)
    from_prev = shifted(window_sum[2 * piece_len :], ("batch", "sub"), 1)
    own_rows = window_sum[piece_len : 2 * piece_len] + from_next + from_prev
    pair_index = jnp.arange(left_slots.shape[1], dtype=jnp.int32)
    left_active = pair_index < share_count[0, 0]
    right_active = pair_index < share_count[0, 1]
    forward = jnp.where(right_active, own_rows[right_slots[0]], 0.0)
    backward = jnp.where(left_active, own_rows[left_slots[0]], 0.0)
    from_left = passed_along(forward, "dom", 1)
    from_right = passed_along(backward, "dom", -1)
    applied = own_rows.at[left_slots[0]].add(jnp.where(left_active, from_left, 0.0))
    applied = applied.at[right_slots[0]].add(jnp.where(right_active, from_right, 0.0))
    owner_mask = (
        jnp.ones((piece_len,), jnp.float32).at[left_slots[0]].set(jnp.where(left_active, 0.0, 1.0))
    )
    scaled = owner_mask * inverse_diagonal
    partial = jnp.stack(
        [
            jnp.sum(scaled * residual * residual),
            jnp.sum(owner_mask * direction * applied),
            jnp.sum(scaled * residual * applied),
            jnp.sum(scaled * applied * applied),
        ]
    )
    total = summed(partial, ("sub", "batch", "dom"))
    old_norm, curvature, cross, square = (total[i] for i in range(4))
    step_size = old_norm / curvature
    new_solution = solution + step_size * direction
    new_residual = residual - step_size * applied
    precond = inverse_diagonal * new_residual
    new_norm = old_norm - step_size * (2.0 * cross - step_size * square)
    new_direction = precond + new_norm / old_norm * direction
    return (new_solution, new_residual, new_direction)


def solution(mesh):
    return jax.shard_map(
        local,
        mesh=mesh,
        in_specs=(
            P(("groups", "dom", "batch", "sub")),
            P(("groups", "dom", "batch", "sub")),
            P(("groups", "dom", "batch", "sub")),
            P(("groups", "dom", "batch", "sub")),
            P(("groups", "dom", "batch", "sub"), None, None),
            P(("groups", "dom", "batch", "sub"), None),
            P(("groups", "dom", "batch", "sub")),
            P(("groups", "dom", "batch", "sub"), None),
            P(("groups", "dom", "batch", "sub"), None),
            P(("groups", "dom", "batch", "sub"), None),
        ),
        out_specs=(
            P(("groups", "dom", "batch", "sub")),
            P(("groups", "dom", "batch", "sub")),
            P(("groups", "dom", "batch", "sub")),
        ),
        check_vma=False,
    )
```

```python
import functools

import jax
import jax.numpy as jnp
from jax import lax
from jax.experimental import pallas as pl
from jax.experimental.pallas import tpu as pltpu
from jax.sharding import PartitionSpec as P

ORDER = 10
LANES = 128
VMEM_LIMIT = 32 * 1024 * 1024
SUMS = 24
STATIC = 48


def split(value):
    high = value.astype(jnp.bfloat16).astype(jnp.float32)
    rest = value - high
    middle = rest.astype(jnp.bfloat16).astype(jnp.float32)
    return [high, middle, rest - middle]


def half(value):
    return value.astype(jnp.bfloat16)


def pick(table, lane_hot, row_hot):
    rows = table.shape[0]
    parts = jnp.dot(
        half(jnp.concatenate(split(table), axis=0)), lane_hot, preferred_element_type=jnp.float32
    )
    found = (parts[:rows] + parts[rows : 2 * rows]) + parts[2 * rows :]
    return jnp.sum(found * row_hot, axis=0, keepdims=True)


def place(values, lane_hot, row_hot):
    rows = row_hot.shape[0]
    spread = jnp.concatenate([row_hot * part for part in split(values)], axis=0)
    parts = lax.dot_general(
        half(spread), lane_hot, (((1,), (1,)), ((), ())), preferred_element_type=jnp.float32
    )
    return (parts[:rows] + parts[rows : 2 * rows]) + parts[2 * rows :]


def hot(index, count):
    rows = lax.broadcasted_iota(jnp.int32, (count, index.shape[1]), 0)
    return jnp.where(rows == index, 1.0, 0.0)


def as_rows(row):
    return [row[:, i * LANES : (i + 1) * LANES] for i in range(row.shape[1] // LANES)]


def as_row(rows):
    return jnp.concatenate([rows[i : i + 1] for i in range(rows.shape[0])], axis=1)


def prepare_kernel(
    group_axes,
    order_ref,
    count_ref,
    dofs_ref,
    left_ref,
    right_ref,
    direction_ref,
    residual_ref,
    diagonal_ref,
    blocks_hbm,
    blocks_ref,
    lane_ref,
    row_ref,
    pair_lane_ref,
    pair_row_ref,
    static_ref,
    index_ref,
    sem,
):
    copy = pltpu.make_async_copy(blocks_hbm, blocks_ref, sem)
    copy.start()
    (outer, inner) = group_axes
    me = lax.axis_index(outer) * lax.axis_size(inner) + lax.axis_index(inner)
    elements, size = dofs_ref.shape
    width = index_ref.shape[1]
    rows = direction_ref.shape[0]
    slot_bits = (rows * LANES - 1).bit_length()
    lane_bits = LANES.bit_length() - 1
    index_ref[...] = jnp.full(index_ref.shape, -1, jnp.int32)
    index_ref[:elements, :size] = dofs_ref[...]
    lanes = lax.broadcasted_iota(jnp.int32, (1, width), 1)
    for e in range(elements):
        order = order_ref[e]
        live = size * (6 * order * order + 2) // (6 * ORDER * ORDER + 2)
        active = lanes < live
        dofs = index_ref[e : e + 1, :]
        piece = lax.shift_right_logical(dofs, slot_bits)
        place_of = jnp.where(piece == me, 0, jnp.where(piece == (me ^ 1), 1, 2))
        high = place_of * rows + (lax.shift_right_logical(dofs, lane_bits) & (rows - 1))
        low = jnp.where(active, dofs & (LANES - 1), -1)
        high = jnp.where(active, high, -1)
        lane_ref[:, e * width : (e + 1) * width] = half(hot(low, LANES))
        row_ref[:, e * width : (e + 1) * width] = hot(high, 3 * rows)
    pairs = left_ref.shape[1]
    pair_lanes = lax.broadcasted_iota(jnp.int32, (1, pairs), 1)
    right = jnp.where(pair_lanes < count_ref[0, 1], right_ref[...], -1)
    left = jnp.where(pair_lanes < count_ref[0, 0], left_ref[...], -1)
    slots = jnp.concatenate([right, left], axis=1)
    pair_lane = half(hot(jnp.where(slots < 0, -1, slots & (LANES - 1)), LANES))
    pair_row = hot(lax.shift_right_arithmetic(slots, lane_bits), rows)
    pair_lane_ref[...] = pair_lane
    pair_row_ref[...] = pair_row
    shared = lax.dot_general(
        half(pair_row[:, pairs:]),
        pair_lane[:, pairs:],
        (((1,), (1,)), ((), ())),
        preferred_element_type=jnp.float32,
    )
    owner = 1.0 - shared
    direction = direction_ref[...]
    diagonal = diagonal_ref[...]
    scaled = diagonal * residual_ref[...]
    static_ref[0:8] = owner * diagonal
    static_ref[8:16] = owner * direction
    static_ref[16:24] = owner * scaled
    static_ref[24:32] = owner * scaled * residual_ref[...]
    lines = []
    for table in (direction, scaled, diagonal):
        lines += as_rows(pick(table, pair_lane[:, :pairs], pair_row[:, :pairs]))
    lines += as_rows(slots.astype(jnp.float32))
    lines += [jnp.zeros((1, LANES), jnp.float32)] * (STATIC - 32 - len(lines))
    static_ref[32:STATIC] = jnp.concatenate(lines, axis=0)
    copy.wait()


def element_kernel(
    own_ref, first_ref, second_ref, blocks_ref, lane_ref, row_ref, static_ref, out_ref, in_ref, y_ref
):
    elements, size, _ = blocks_ref.shape
    width = y_ref.shape[1]
    window = jnp.concatenate([own_ref[...], first_ref[...], second_ref[...]], axis=0)
    element_in = pick(window, lane_ref[...], row_ref[...])
    in_ref[...] = jnp.zeros(in_ref.shape, jnp.float32)
    for e in range(elements):
        in_ref[e : e + 1, :] = element_in[:, e * width : (e + 1) * width]
    columns = in_ref[...].T
    y_ref[...] = jnp.zeros(y_ref.shape, jnp.float32)
    whole = size // 8 * 8
    for e in range(elements):
        total = jnp.zeros((8, size), jnp.float32)
        for start in range(0, whole, 8):
            total += blocks_ref[e, start : start + 8, :] * columns[start : start + 8, e : e + 1]
        total = jnp.sum(total, axis=0, keepdims=True)
        for line in range(whole, size):
            total += blocks_ref[e, line : line + 1, :] * columns[line : line + 1, e : e + 1]
        y_ref[e : e + 1, :size] = total
    element_out = jnp.concatenate([y_ref[e : e + 1, :] for e in range(elements)], axis=1)
    out_ref[:SUMS] = place(element_out, lane_ref[...], row_ref[...])
    out_ref[SUMS:] = static_ref[...]


def sum_kernel(count, *refs):
    messages, (pair_lane_ref, pair_row_ref, own_ref, out_ref) = refs[:count], refs[count:]
    rows = own_ref.shape[0]
    half_pairs = pair_lane_ref.shape[1] // 2
    lines = half_pairs // LANES
    lane_bits = LANES.bit_length() - 1
    totals = [jnp.zeros((rows, LANES), jnp.float32) for _ in range(4)]
    found = [[] for _ in range(5)]
    for m, message in enumerate(messages):
        applied = message[0:8] + messages[m ^ 1][8:16] + messages[m ^ 3][16:24]
        at = functools.partial(lambda ref, i: ref[SUMS + 8 * i : SUMS + 8 * i + 8], message)
        totals[0] += at(3)
        totals[1] += at(1) * applied
        totals[2] += at(2) * applied
        totals[3] += at(0) * applied * applied
        base = SUMS + 32
        if m == 0:
            own_ref[...] = applied
            pair_lane, pair_row = pair_lane_ref[...], pair_row_ref[...]
        else:
            slots = as_row(message[base + 3 * lines : base + 5 * lines]).astype(jnp.int32)
            pair_lane = half(hot(jnp.where(slots < 0, -1, slots & (LANES - 1)), LANES))
            pair_row = hot(lax.shift_right_arithmetic(slots, lane_bits), rows)
        values = as_rows(pick(applied, pair_lane, pair_row))
        found[0] += values[:lines]
        found[1] += values[lines:]
        for i in range(3):
            found[2 + i].append(message[base + i * lines : base + (i + 1) * lines])
    for i in range(4):
        out_ref[i * rows : (i + 1) * rows] = totals[i]
    base, step = 4 * rows, count * lines
    for i in range(5):
        out_ref[base + i * step : base + (i + 1) * step] = jnp.concatenate(found[i], axis=0)


def final_kernel(
    dom_axis,
    inner_axis,
    ordered,
    count,
    lines,
    *refs,
):
    messages = [ref[...] for ref in refs[:count]]
    (
        own_ref,
        pair_lane_ref,
        pair_row_ref,
        solution_ref,
        residual_ref,
        direction_ref,
        diagonal_ref,
        new_solution_ref,
        new_residual_ref,
        new_direction_ref,
    ) = refs[count:]
    rows = own_ref.shape[0]
    me = lax.axis_index(dom_axis)
    if not ordered:
        own, direct, far, relayed = messages
        relayed = other_order(relayed, 4 * rows, lines)
        even = lax.axis_index(inner_axis) == 0
        line = [own, jnp.where(even, direct, relayed), jnp.where(even, relayed, direct), far]
        low = (me & 1) == 0
        high = (me & 2) == 0
        line = [jnp.where(low, line[i], line[i ^ 1]) for i in range(4)]
        messages = [jnp.where(high, line[i], line[i ^ 2]) for i in range(4)]
    base = 4 * rows
    step = (messages[0].shape[0] - base) // 5
    totals = messages[0][:base]
    for message in messages[1:]:
        totals = totals + message[:base]
    old, curve, cross, square = (totals[i * rows : (i + 1) * rows] for i in range(4))

    def part(message, i):
        return message[base + i * step : base + (i + 1) * step]

    from_left = jnp.zeros((lines, LANES), jnp.float32)
    from_right = jnp.zeros((lines, LANES), jnp.float32)
    for d in range(count - 1):
        near, next_one = messages[d], messages[d + 1]
        forward, backward = part(near, 0), part(next_one, 1)
        terms = [
            part(near, 2) * backward,
            part(near, 3) * backward,
            part(near, 4) * backward * (2.0 * forward + backward),
        ]
        for start in range(0, step, rows):
            curve = curve + terms[0][start : start + rows]
            cross = cross + terms[1][start : start + rows]
            square = square + terms[2][start : start + rows]
        from_left = jnp.where(me == d + 1, forward[:lines], from_left)
        from_right = jnp.where(me == d, backward[:lines], from_right)
    incoming = as_row(jnp.concatenate([from_right, from_left], axis=0))
    applied = own_ref[...] + place(incoming, pair_lane_ref[...], pair_row_ref[...])

    def whole(value):
        return jnp.sum(value, axis=(0, 1), keepdims=True)

    old_norm = whole(old)
    step_size = old_norm / whole(curve)
    new_norm = whole(old - step_size * (2.0 * cross - step_size * square))
    direction = direction_ref[...]
    new_residual = residual_ref[...] - step_size * applied
    new_solution_ref[...] = solution_ref[...] + step_size * direction
    new_residual_ref[...] = new_residual
    new_direction_ref[...] = diagonal_ref[...] * new_residual + (new_norm / old_norm) * direction


def other_order(message, base, lines):
    blocks = [message[:base]]
    for start in range(base, message.shape[0], 2 * lines):
        blocks += [message[start + lines : start + 2 * lines], message[start : start + lines]]
    return jnp.concatenate(blocks, axis=0)


def specs(spaces):
    return [pl.BlockSpec(memory_space=space) for space in spaces]


def swap_first(count):
    return [(i, i ^ 1) for i in range(count)]


def swap_second(count):
    return [(i, (i + 1 if i % 2 else i - 1) % count) for i in range(count)]


def local(
    solution,
    residual,
    direction,
    inverse_diagonal,
    schur_blocks,
    elem_dofs,
    element_order,
    left_slots,
    right_slots,
    share_count,
):
    group, dom = ("batch", "sub"), "dom"
    group_count, dom_count = lax.axis_size(group), lax.axis_size(dom)
    sub_count = lax.axis_size("sub")
    elements, size = elem_dofs.shape
    width = -(-size // LANES) * LANES
    pairs = left_slots.shape[1]
    lines = pairs // LANES
    rows = residual.shape[0] // LANES
    f32, bf16 = jnp.float32, jnp.bfloat16
    vmem, smem = pltpu.VMEM, pltpu.SMEM
    params = pltpu.CompilerParams(vmem_limit_bytes=VMEM_LIMIT)

    solution, residual, direction, inverse_diagonal = (
        value.reshape(rows, LANES) for value in (solution, residual, direction, inverse_diagonal)
    )
    first = lax.ppermute(direction, group, swap_first(group_count))
    second = lax.ppermute(direction, group, swap_second(group_count))

    blocks, lane_hot, row_hot, pair_lane, pair_row, static = pl.pallas_call(
        functools.partial(prepare_kernel, group),
        out_shape=[
            jax.ShapeDtypeStruct(schur_blocks.shape, f32),
            jax.ShapeDtypeStruct((LANES, elements * width), bf16),
            jax.ShapeDtypeStruct((3 * rows, elements * width), f32),
            jax.ShapeDtypeStruct((LANES, 2 * pairs), bf16),
            jax.ShapeDtypeStruct((rows, 2 * pairs), f32),
            jax.ShapeDtypeStruct((STATIC, LANES), f32),
        ],
        in_specs=specs([smem, smem] + [vmem] * 6 + [pl.ANY]),
        out_specs=specs([vmem] * 6),
        scratch_shapes=[pltpu.VMEM((8, width), jnp.int32), pltpu.SemaphoreType.DMA],
        compiler_params=params,
        name="prepare",
    )(
        element_order,
        share_count,
        elem_dofs,
        left_slots,
        right_slots,
        direction,
        residual,
        inverse_diagonal,
        schur_blocks,
    )

    message = pl.pallas_call(
        element_kernel,
        out_shape=jax.ShapeDtypeStruct((SUMS + STATIC, LANES), f32),
        in_specs=specs([vmem] * 7),
        out_specs=pl.BlockSpec(memory_space=vmem),
        scratch_shapes=[pltpu.VMEM((8, width), f32), pltpu.VMEM((8, width), f32)],
        compiler_params=params,
        name="elements",
    )(direction, first, second, blocks, lane_hot, row_hot, static)

    if group_count == 4:
        messages = [message] + [
            lax.ppermute(message, group, [(i, i ^ m) for i in range(4)]) for m in (1, 2, 3)
        ]
    else:
        me = lax.axis_index(group)
        order = me ^ jnp.arange(group_count)
        everyone = lax.all_gather(message, group)
        second_of = jnp.array([target for _, target in swap_second(group_count)])
        moved = everyone[second_of[me ^ 3 ^ jnp.arange(group_count)], 2 * rows : 3 * rows]
        everyone = everyone[order].at[:, 2 * rows : 3 * rows].set(moved)
        messages = [everyone[m] for m in range(group_count)]

    own, message = pl.pallas_call(
        functools.partial(sum_kernel, group_count),
        out_shape=[
            jax.ShapeDtypeStruct((rows, LANES), f32),
            jax.ShapeDtypeStruct((4 * rows + 5 * group_count * lines, LANES), f32),
        ],
        in_specs=specs([vmem] * (group_count + 2)),
        out_specs=specs([vmem] * 2),
        compiler_params=params,
        name="sums",
    )(*messages, pair_lane, pair_row)

    ordered = not (dom_count == 4 and sub_count == 2)
    if ordered:
        everyone = lax.all_gather(message, dom)
        messages = [everyone[d] for d in range(dom_count)]
    else:
        line = (dom, "sub")
        near = [(2 * d + s, 2 * (d ^ (1 + s)) + s) for d in range(4) for s in range(2)]
        opposite = [(2 * d + s, 2 * (d ^ 3) + s) for d in range(4) for s in range(2)]
        direct = lax.ppermute(message, line, near)
        far = lax.ppermute(message, line, opposite)
        relayed = lax.ppermute(direct, "sub", [(0, 1), (1, 0)])
        messages = [message, direct, far, relayed]

    outputs = pl.pallas_call(
        functools.partial(final_kernel, dom, "sub", ordered, dom_count, lines),
        out_shape=[jax.ShapeDtypeStruct((rows, LANES), f32)] * 3,
        in_specs=specs([vmem] * (dom_count + 7)),
        out_specs=specs([vmem] * 3),
        compiler_params=params,
        name="update",
    )(*messages, own, pair_lane, pair_row, solution, residual, direction, inverse_diagonal)
    return tuple(value.reshape(-1) for value in outputs)


def solution(mesh):
    whole = P(("groups", "dom", "batch", "sub"))
    lines = P(("groups", "dom", "batch", "sub"), None)
    return jax.shard_map(
        local,
        mesh=mesh,
        in_specs=(whole,) * 4
        + (P(("groups", "dom", "batch", "sub"), None, None), lines, whole, lines, lines, lines),
        out_specs=(whole,) * 3,
        check_vma=False,
    )
```

```python
import functools

import jax
import jax.numpy as jnp
from jax import lax
from jax.experimental import pallas as pl
from jax.experimental.pallas import tpu as pltpu
from jax.sharding import PartitionSpec as P

ORDER = 10
LANES = 128
VMEM_LIMIT = 32 * 1024 * 1024
SUMS = 24
STATIC = 48


def split(value):
    high = value.astype(jnp.bfloat16).astype(jnp.float32)
    rest = value - high
    middle = rest.astype(jnp.bfloat16).astype(jnp.float32)
    return [high, middle, rest - middle]


def half(value):
    return value.astype(jnp.bfloat16)


def pick(table, lane_hot, row_hot):
    rows = table.shape[0]
    parts = jnp.dot(
        half(jnp.concatenate(split(table), axis=0)), lane_hot, preferred_element_type=jnp.float32
    )
    found = (parts[:rows] + parts[rows : 2 * rows]) + parts[2 * rows :]
    return jnp.sum(found * row_hot, axis=0, keepdims=True)


def place(values, lane_hot, row_hot):
    rows = row_hot.shape[0]
    spread = jnp.concatenate([row_hot * part for part in split(values)], axis=0)
    parts = lax.dot_general(
        half(spread), lane_hot, (((1,), (1,)), ((), ())), preferred_element_type=jnp.float32
    )
    return (parts[:rows] + parts[rows : 2 * rows]) + parts[2 * rows :]


def hot(index, count):
    rows = lax.broadcasted_iota(jnp.int32, (count, index.shape[1]), 0)
    return jnp.where(rows == index, 1.0, 0.0)


def as_rows(row):
    return [row[:, i * LANES : (i + 1) * LANES] for i in range(row.shape[1] // LANES)]


def as_row(rows):
    return jnp.concatenate([rows[i : i + 1] for i in range(rows.shape[0])], axis=1)


def prepare_kernel(
    group_axes,
    order_hbm,
    count_hbm,
    dofs_hbm,
    left_hbm,
    right_hbm,
    solution_hbm,
    residual_hbm,
    direction_hbm,
    diagonal_hbm,
    lane_ref,
    row_ref,
    pair_lane_ref,
    pair_row_ref,
    static_ref,
    vector_ref,
    dofs_ref,
    index_ref,
    left_ref,
    right_ref,
    order_ref,
    count_ref,
    sems,
):
    rows = direction_hbm.shape[0]
    moves = [
        (order_hbm, order_ref),
        (count_hbm, count_ref),
        (dofs_hbm, dofs_ref),
        (left_hbm, left_ref),
        (right_hbm, right_ref),
    ]
    for i, vector in enumerate((solution_hbm, residual_hbm, direction_hbm, diagonal_hbm)):
        moves.append((vector, vector_ref.at[i * rows : (i + 1) * rows]))
    copies = [pltpu.make_async_copy(*move, sems.at[i]) for i, move in enumerate(moves)]
    for copy in copies:
        copy.start()
    (outer, inner) = group_axes
    me = lax.axis_index(outer) * lax.axis_size(inner) + lax.axis_index(inner)
    elements, size = dofs_ref.shape
    width = index_ref.shape[1]
    slot_bits = (rows * LANES - 1).bit_length()
    lane_bits = LANES.bit_length() - 1
    index_ref[...] = jnp.full(index_ref.shape, -1, jnp.int32)
    lanes = lax.broadcasted_iota(jnp.int32, (1, width), 1)
    for copy in copies:
        copy.wait()
    index_ref[:elements, :size] = dofs_ref[...]
    for e in range(elements):
        order = order_ref[e]
        live = size * (6 * order * order + 2) // (6 * ORDER * ORDER + 2)
        active = lanes < live
        dofs = index_ref[e : e + 1, :]
        piece = lax.shift_right_logical(dofs, slot_bits)
        place_of = jnp.where(piece == me, 0, jnp.where(piece == (me ^ 1), 1, 2))
        high = place_of * rows + (lax.shift_right_logical(dofs, lane_bits) & (rows - 1))
        low = jnp.where(active, dofs & (LANES - 1), -1)
        high = jnp.where(active, high, -1)
        lane_ref[:, e * width : (e + 1) * width] = half(hot(low, LANES))
        row_ref[:, e * width : (e + 1) * width] = hot(high, 3 * rows)
    pairs = left_ref.shape[1]
    pair_lanes = lax.broadcasted_iota(jnp.int32, (1, pairs), 1)
    right = jnp.where(pair_lanes < count_ref[0, 1], right_ref[...], -1)
    left = jnp.where(pair_lanes < count_ref[0, 0], left_ref[...], -1)
    slots = jnp.concatenate([right, left], axis=1)
    pair_lane = half(hot(jnp.where(slots < 0, -1, slots & (LANES - 1)), LANES))
    pair_row = hot(lax.shift_right_arithmetic(slots, lane_bits), rows)
    pair_lane_ref[...] = pair_lane
    pair_row_ref[...] = pair_row
    shared = lax.dot_general(
        half(pair_row[:, pairs:]),
        pair_lane[:, pairs:],
        (((1,), (1,)), ((), ())),
        preferred_element_type=jnp.float32,
    )
    owner = 1.0 - shared
    residual = vector_ref[rows : 2 * rows]
    direction = vector_ref[2 * rows : 3 * rows]
    diagonal = vector_ref[3 * rows : 4 * rows]
    scaled = diagonal * residual
    static_ref[0:8] = owner * diagonal
    static_ref[8:16] = owner * direction
    static_ref[16:24] = owner * scaled
    static_ref[24:32] = owner * scaled * residual
    lines = []
    for table in (direction, scaled, diagonal):
        lines += as_rows(pick(table, pair_lane[:, :pairs], pair_row[:, :pairs]))
    lines += as_rows(slots.astype(jnp.float32))
    lines += [jnp.zeros((1, LANES), jnp.float32)] * (STATIC - 32 - len(lines))
    static_ref[32:STATIC] = jnp.concatenate(lines, axis=0)


def element_kernel(
    vector_ref, first_ref, second_ref, blocks_ref, lane_ref, row_ref, static_ref, out_ref, in_ref, y_ref
):
    elements, size, _ = blocks_ref.shape
    width = y_ref.shape[1]
    rows = first_ref.shape[0]
    own = vector_ref[2 * rows : 3 * rows]
    window = jnp.concatenate([own, first_ref[...], second_ref[...]], axis=0)
    element_in = pick(window, lane_ref[...], row_ref[...])
    in_ref[...] = jnp.zeros(in_ref.shape, jnp.float32)
    for e in range(elements):
        in_ref[e : e + 1, :] = element_in[:, e * width : (e + 1) * width]
    columns = in_ref[...].T
    y_ref[...] = jnp.zeros(y_ref.shape, jnp.float32)
    whole = size // 8 * 8
    for e in range(elements):
        total = jnp.zeros((8, size), jnp.float32)
        for start in range(0, whole, 8):
            total += blocks_ref[e, start : start + 8, :] * columns[start : start + 8, e : e + 1]
        total = jnp.sum(total, axis=0, keepdims=True)
        for line in range(whole, size):
            total += blocks_ref[e, line : line + 1, :] * columns[line : line + 1, e : e + 1]
        y_ref[e : e + 1, :size] = total
    element_out = jnp.concatenate([y_ref[e : e + 1, :] for e in range(elements)], axis=1)
    out_ref[:SUMS] = place(element_out, lane_ref[...], row_ref[...])
    out_ref[SUMS:] = static_ref[...]


def sum_kernel(count, *refs):
    messages, (pair_lane_ref, pair_row_ref, own_ref, out_ref) = refs[:count], refs[count:]
    rows = own_ref.shape[0]
    half_pairs = pair_lane_ref.shape[1] // 2
    lines = half_pairs // LANES
    lane_bits = LANES.bit_length() - 1
    totals = [jnp.zeros((rows, LANES), jnp.float32) for _ in range(4)]
    found = [[] for _ in range(5)]
    for m, message in enumerate(messages):
        applied = message[0:8] + messages[m ^ 1][8:16] + messages[m ^ 3][16:24]
        at = functools.partial(lambda ref, i: ref[SUMS + 8 * i : SUMS + 8 * i + 8], message)
        totals[0] += at(3)
        totals[1] += at(1) * applied
        totals[2] += at(2) * applied
        totals[3] += at(0) * applied * applied
        base = SUMS + 32
        if m == 0:
            own_ref[...] = applied
            pair_lane, pair_row = pair_lane_ref[...], pair_row_ref[...]
        else:
            slots = as_row(message[base + 3 * lines : base + 5 * lines]).astype(jnp.int32)
            pair_lane = half(hot(jnp.where(slots < 0, -1, slots & (LANES - 1)), LANES))
            pair_row = hot(lax.shift_right_arithmetic(slots, lane_bits), rows)
        values = as_rows(pick(applied, pair_lane, pair_row))
        found[0] += values[:lines]
        found[1] += values[lines:]
        for i in range(3):
            found[2 + i].append(message[base + i * lines : base + (i + 1) * lines])
    for i in range(4):
        out_ref[i * rows : (i + 1) * rows] = totals[i]
    base, step = 4 * rows, count * lines
    for i in range(5):
        out_ref[base + i * step : base + (i + 1) * step] = jnp.concatenate(found[i], axis=0)


def final_kernel(
    dom_axis,
    inner_axis,
    ordered,
    count,
    lines,
    *refs,
):
    messages = [ref[...] for ref in refs[:count]]
    (
        own_ref,
        pair_lane_ref,
        pair_row_ref,
        vector_ref,
        new_solution_ref,
        new_residual_ref,
        new_direction_ref,
    ) = refs[count:]
    rows = own_ref.shape[0]
    me = lax.axis_index(dom_axis)
    if not ordered:
        own, direct, far, relayed = messages
        relayed = other_order(relayed, 4 * rows, lines)
        even = lax.axis_index(inner_axis) == 0
        line = [own, jnp.where(even, direct, relayed), jnp.where(even, relayed, direct), far]
        low = (me & 1) == 0
        high = (me & 2) == 0
        line = [jnp.where(low, line[i], line[i ^ 1]) for i in range(4)]
        messages = [jnp.where(high, line[i], line[i ^ 2]) for i in range(4)]
    base = 4 * rows
    step = (messages[0].shape[0] - base) // 5
    totals = messages[0][:base]
    for message in messages[1:]:
        totals = totals + message[:base]
    old, curve, cross, square = (totals[i * rows : (i + 1) * rows] for i in range(4))

    def part(message, i):
        return message[base + i * step : base + (i + 1) * step]

    from_left = jnp.zeros((lines, LANES), jnp.float32)
    from_right = jnp.zeros((lines, LANES), jnp.float32)
    for d in range(count - 1):
        near, next_one = messages[d], messages[d + 1]
        forward, backward = part(near, 0), part(next_one, 1)
        terms = [
            part(near, 2) * backward,
            part(near, 3) * backward,
            part(near, 4) * backward * (2.0 * forward + backward),
        ]
        for start in range(0, step, rows):
            curve = curve + terms[0][start : start + rows]
            cross = cross + terms[1][start : start + rows]
            square = square + terms[2][start : start + rows]
        from_left = jnp.where(me == d + 1, forward[:lines], from_left)
        from_right = jnp.where(me == d, backward[:lines], from_right)
    incoming = as_row(jnp.concatenate([from_right, from_left], axis=0))
    applied = own_ref[...] + place(incoming, pair_lane_ref[...], pair_row_ref[...])

    def whole(value):
        return jnp.sum(value, axis=(0, 1), keepdims=True)

    old_norm = whole(old)
    step_size = old_norm / whole(curve)
    new_norm = whole(old - step_size * (2.0 * cross - step_size * square))
    solution, residual, direction, diagonal = (
        vector_ref[i * rows : (i + 1) * rows] for i in range(4)
    )
    new_residual = residual - step_size * applied
    new_solution_ref[...] = solution + step_size * direction
    new_residual_ref[...] = new_residual
    new_direction_ref[...] = diagonal * new_residual + (new_norm / old_norm) * direction


def other_order(message, base, lines):
    blocks = [message[:base]]
    for start in range(base, message.shape[0], 2 * lines):
        blocks += [message[start + lines : start + 2 * lines], message[start : start + lines]]
    return jnp.concatenate(blocks, axis=0)


def specs(spaces):
    return [pl.BlockSpec(memory_space=space) for space in spaces]


def swap_first(count):
    return [(i, i ^ 1) for i in range(count)]


def swap_second(count):
    return [(i, (i + 1 if i % 2 else i - 1) % count) for i in range(count)]


def local(
    solution,
    residual,
    direction,
    inverse_diagonal,
    schur_blocks,
    elem_dofs,
    element_order,
    left_slots,
    right_slots,
    share_count,
):
    group, dom = ("batch", "sub"), "dom"
    group_count, dom_count = lax.axis_size(group), lax.axis_size(dom)
    sub_count = lax.axis_size("sub")
    elements, size = elem_dofs.shape
    width = -(-size // LANES) * LANES
    pairs = left_slots.shape[1]
    lines = pairs // LANES
    rows = residual.shape[0] // LANES
    f32, bf16 = jnp.float32, jnp.bfloat16
    vmem = pltpu.VMEM
    params = pltpu.CompilerParams(vmem_limit_bytes=VMEM_LIMIT)

    solution, residual, direction, inverse_diagonal = (
        value.reshape(rows, LANES) for value in (solution, residual, direction, inverse_diagonal)
    )
    first = lax.ppermute(direction, group, swap_first(group_count))
    second = lax.ppermute(direction, group, swap_second(group_count))

    lane_hot, row_hot, pair_lane, pair_row, static, vectors = pl.pallas_call(
        functools.partial(prepare_kernel, group),
        out_shape=[
            jax.ShapeDtypeStruct((LANES, elements * width), bf16),
            jax.ShapeDtypeStruct((3 * rows, elements * width), f32),
            jax.ShapeDtypeStruct((LANES, 2 * pairs), bf16),
            jax.ShapeDtypeStruct((rows, 2 * pairs), f32),
            jax.ShapeDtypeStruct((STATIC, LANES), f32),
            jax.ShapeDtypeStruct((4 * rows, LANES), f32),
        ],
        in_specs=specs([pltpu.HBM] * 9),
        out_specs=specs([vmem] * 6),
        scratch_shapes=[
            pltpu.VMEM((elements, size), jnp.int32),
            pltpu.VMEM((8, width), jnp.int32),
            pltpu.VMEM((1, pairs), jnp.int32),
            pltpu.VMEM((1, pairs), jnp.int32),
            pltpu.SMEM((elements,), jnp.int32),
            pltpu.SMEM((1, 2), jnp.int32),
            pltpu.SemaphoreType.DMA((9,)),
        ],
        compiler_params=params,
        cost_estimate=pl.CostEstimate(flops=1600000000, bytes_accessed=16000000, transcendentals=0),
        name="prepare",
    )(
        *(
            pltpu.with_memory_space_constraint(value, pltpu.HBM)
            for value in (
                element_order,
                share_count,
                elem_dofs,
                left_slots,
                right_slots,
                solution,
                residual,
                direction,
                inverse_diagonal,
            )
        )
    )

    message = pl.pallas_call(
        element_kernel,
        out_shape=jax.ShapeDtypeStruct((SUMS + STATIC, LANES), f32),
        in_specs=specs([vmem] * 7),
        out_specs=pl.BlockSpec(memory_space=vmem),
        scratch_shapes=[pltpu.VMEM((8, width), f32), pltpu.VMEM((8, width), f32)],
        compiler_params=params,
        name="elements",
    )(vectors, first, second, schur_blocks, lane_hot, row_hot, static)

    if group_count == 4:
        messages = [message] + [
            lax.ppermute(message, group, [(i, i ^ m) for i in range(4)]) for m in (1, 2, 3)
        ]
    else:
        me = lax.axis_index(group)
        order = me ^ jnp.arange(group_count)
        everyone = lax.all_gather(message, group)
        second_of = jnp.array([target for _, target in swap_second(group_count)])
        moved = everyone[second_of[me ^ 3 ^ jnp.arange(group_count)], 2 * rows : 3 * rows]
        everyone = everyone[order].at[:, 2 * rows : 3 * rows].set(moved)
        messages = [everyone[m] for m in range(group_count)]

    own, message = pl.pallas_call(
        functools.partial(sum_kernel, group_count),
        out_shape=[
            jax.ShapeDtypeStruct((rows, LANES), f32),
            jax.ShapeDtypeStruct((4 * rows + 5 * group_count * lines, LANES), f32),
        ],
        in_specs=specs([vmem] * (group_count + 2)),
        out_specs=specs([vmem] * 2),
        compiler_params=params,
        name="sums",
    )(*messages, pair_lane, pair_row)

    ordered = not (dom_count == 4 and sub_count == 2)
    if ordered:
        everyone = lax.all_gather(message, dom)
        messages = [everyone[d] for d in range(dom_count)]
    else:
        line = (dom, "sub")
        near = [(2 * d + s, 2 * (d ^ (1 + s)) + s) for d in range(4) for s in range(2)]
        opposite = [(2 * d + s, 2 * (d ^ 3) + s) for d in range(4) for s in range(2)]
        direct = lax.ppermute(message, line, near)
        far = lax.ppermute(message, line, opposite)
        relayed = lax.ppermute(direct, "sub", [(0, 1), (1, 0)])
        messages = [message, direct, far, relayed]

    outputs = pl.pallas_call(
        functools.partial(final_kernel, dom, "sub", ordered, dom_count, lines),
        out_shape=[jax.ShapeDtypeStruct((rows, LANES), f32)] * 3,
        in_specs=specs([vmem] * (dom_count + 4)),
        out_specs=specs([vmem] * 3),
        compiler_params=params,
        name="update",
    )(*messages, own, pair_lane, pair_row, vectors)
    return tuple(value.reshape(-1) for value in outputs)


def solution(mesh):
    whole = P(("groups", "dom", "batch", "sub"))
    lines = P(("groups", "dom", "batch", "sub"), None)
    return jax.shard_map(
        local,
        mesh=mesh,
        in_specs=(whole,) * 4
        + (P(("groups", "dom", "batch", "sub"), None, None), lines, whole, lines, lines, lines),
        out_specs=(whole,) * 3,
        check_vma=False,
    )
```

```python
import functools

import jax
import jax.numpy as jnp
from jax import lax
from jax.experimental import pallas as pl
from jax.experimental.pallas import tpu as pltpu
from jax.sharding import PartitionSpec as P

ORDER = 10
LANES = 128
VMEM_LIMIT = 32 * 1024 * 1024
SUMS = 24
STATIC = 40
SPLIT, BOTH = (2, 3), 1
TOTALS = 8


def split(value):
    high = value.astype(jnp.bfloat16).astype(jnp.float32)
    rest = value - high
    middle = rest.astype(jnp.bfloat16).astype(jnp.float32)
    return [high, middle, rest - middle]


def half(value):
    return value.astype(jnp.bfloat16)


def pick(table, lane_hot, row_hot):
    rows = table.shape[0]
    parts = jnp.dot(
        half(jnp.concatenate(split(table), axis=0)), lane_hot, preferred_element_type=jnp.float32
    )
    found = (parts[:rows] + parts[rows : 2 * rows]) + parts[2 * rows :]
    return jnp.sum(found * row_hot, axis=0, keepdims=True)


def place(values, lane_hot, row_hot):
    rows = row_hot.shape[0]
    spread = jnp.concatenate([row_hot * part for part in split(values)], axis=0)
    parts = lax.dot_general(
        half(spread), lane_hot, (((1,), (1,)), ((), ())), preferred_element_type=jnp.float32
    )
    return (parts[:rows] + parts[rows : 2 * rows]) + parts[2 * rows :]


def hot(index, count):
    rows = lax.broadcasted_iota(jnp.int32, (count, index.shape[1]), 0)
    return jnp.where(rows == index, 1.0, 0.0)


def as_rows(row):
    return [row[:, i * LANES : (i + 1) * LANES] for i in range(row.shape[1] // LANES)]


def as_row(rows):
    return jnp.concatenate([rows[i : i + 1] for i in range(rows.shape[0])], axis=1)


def prepare_kernel(
    group_axes,
    order_hbm,
    count_hbm,
    dofs_hbm,
    left_hbm,
    right_hbm,
    solution_hbm,
    residual_hbm,
    direction_hbm,
    diagonal_hbm,
    lane_ref,
    row_ref,
    pair_lane_ref,
    pair_row_ref,
    static_ref,
    vector_ref,
    dofs_ref,
    index_ref,
    left_ref,
    right_ref,
    order_ref,
    count_ref,
    sems,
):
    rows = direction_hbm.shape[0]
    moves = [
        (order_hbm, order_ref),
        (count_hbm, count_ref),
        (dofs_hbm, dofs_ref),
        (left_hbm, left_ref),
        (right_hbm, right_ref),
    ]
    for i, vector in enumerate((solution_hbm, residual_hbm, direction_hbm, diagonal_hbm)):
        moves.append((vector, vector_ref.at[i * rows : (i + 1) * rows]))
    copies = [pltpu.make_async_copy(*move, sems.at[i]) for i, move in enumerate(moves)]
    for copy in copies:
        copy.start()
    (outer, inner) = group_axes
    me = lax.axis_index(outer) * lax.axis_size(inner) + lax.axis_index(inner)
    elements, size = dofs_ref.shape
    width = index_ref.shape[1]
    slot_bits = (rows * LANES - 1).bit_length()
    lane_bits = LANES.bit_length() - 1
    index_ref[...] = jnp.full(index_ref.shape, -1, jnp.int32)
    lanes = lax.broadcasted_iota(jnp.int32, (1, width), 1)
    for copy in copies:
        copy.wait()
    index_ref[:elements, :size] = dofs_ref[...]
    for e in range(elements):
        order = order_ref[e]
        live = size * (6 * order * order + 2) // (6 * ORDER * ORDER + 2)
        active = lanes < live
        dofs = index_ref[e : e + 1, :]
        piece = lax.shift_right_logical(dofs, slot_bits)
        place_of = jnp.where(piece == me, 0, jnp.where(piece == (me ^ 1), 1, 2))
        high = place_of * rows + (lax.shift_right_logical(dofs, lane_bits) & (rows - 1))
        low = jnp.where(active, dofs & (LANES - 1), -1)
        high = jnp.where(active, high, -1)
        lane_ref[:, e * width : (e + 1) * width] = half(hot(low, LANES))
        row_ref[:, e * width : (e + 1) * width] = hot(high, 3 * rows)
    pairs = left_ref.shape[1]
    pair_lanes = lax.broadcasted_iota(jnp.int32, (1, pairs), 1)
    right = jnp.where(pair_lanes < count_ref[0, 1], right_ref[...], -1)
    left = jnp.where(pair_lanes < count_ref[0, 0], left_ref[...], -1)
    slots = jnp.concatenate([right, left], axis=1)
    pair_lane = half(hot(jnp.where(slots < 0, -1, slots & (LANES - 1)), LANES))
    pair_row = hot(lax.shift_right_arithmetic(slots, lane_bits), rows)
    pair_lane_ref[...] = pair_lane
    pair_row_ref[...] = pair_row
    shared = lax.dot_general(
        half(pair_row[:, pairs:]),
        pair_lane[:, pairs:],
        (((1,), (1,)), ((), ())),
        preferred_element_type=jnp.float32,
    )
    owner = 1.0 - shared
    residual = vector_ref[rows : 2 * rows]
    direction = vector_ref[2 * rows : 3 * rows]
    diagonal = vector_ref[3 * rows : 4 * rows]
    scaled = diagonal * residual
    static_ref[0:8] = owner * diagonal
    static_ref[8:16] = owner * direction
    static_ref[16:24] = owner * scaled
    lines = [jnp.sum(owner * scaled * residual, axis=0, keepdims=True)]
    for table in (direction, scaled, diagonal):
        lines += as_rows(pick(table, pair_lane[:, :pairs], pair_row[:, :pairs]))
    lines += as_rows(slots.astype(jnp.float32))
    lines += [jnp.zeros((1, LANES), jnp.float32)] * (STATIC - 24 - len(lines))
    static_ref[24:STATIC] = jnp.concatenate(lines, axis=0)


def element_kernel(
    vector_ref, first_ref, second_ref, blocks_ref, lane_ref, row_ref, static_ref, out_ref, in_ref, y_ref
):
    elements, size, _ = blocks_ref.shape
    width = y_ref.shape[1]
    rows = first_ref.shape[0]
    own = vector_ref[2 * rows : 3 * rows]
    window = jnp.concatenate([own, first_ref[...], second_ref[...]], axis=0)
    element_in = pick(window, lane_ref[...], row_ref[...])
    in_ref[...] = jnp.zeros(in_ref.shape, jnp.float32)
    for e in range(elements):
        in_ref[e : e + 1, :] = element_in[:, e * width : (e + 1) * width]
    columns = in_ref[...].T
    y_ref[...] = jnp.zeros(y_ref.shape, jnp.float32)
    whole = size // 8 * 8
    for e in range(elements):
        total = jnp.zeros((8, size), jnp.float32)
        for start in range(0, whole, 8):
            total += blocks_ref[e, start : start + 8, :] * columns[start : start + 8, e : e + 1]
        total = jnp.sum(total, axis=0, keepdims=True)
        for line in range(whole, size):
            total += blocks_ref[e, line : line + 1, :] * columns[line : line + 1, e : e + 1]
        y_ref[e : e + 1, :size] = total
    element_out = jnp.concatenate([y_ref[e : e + 1, :] for e in range(elements)], axis=1)
    out_ref[:SUMS] = place(element_out, lane_ref[...], row_ref[...])
    out_ref[SUMS:] = static_ref[...]


def sum_kernel(count, *refs):
    messages, (pair_lane_ref, pair_row_ref, own_ref, out_ref) = refs[:count], refs[count:]
    rows = own_ref.shape[0]
    half_pairs = pair_lane_ref.shape[1] // 2
    lines = half_pairs // LANES
    lane_bits = LANES.bit_length() - 1
    totals = [jnp.zeros((rows, LANES), jnp.float32) for _ in range(3)]
    old = jnp.zeros((1, LANES), jnp.float32)
    found = [[] for _ in range(5)]
    for m, message in enumerate(messages):
        applied = message[0:8] + messages[m ^ 1][8:16] + messages[m ^ 3][16:24]
        at = functools.partial(lambda ref, i: ref[SUMS + 8 * i : SUMS + 8 * i + 8], message)
        totals[0] += at(1) * applied
        totals[1] += at(2) * applied
        totals[2] += at(0) * applied * applied
        base = SUMS + 24
        old += message[base : base + 1]
        base += 1
        if m == 0:
            own_ref[...] = applied
            pair_lane, pair_row = pair_lane_ref[...], pair_row_ref[...]
        else:
            slots = as_row(message[base + 3 * lines : base + 5 * lines]).astype(jnp.int32)
            pair_lane = half(hot(jnp.where(slots < 0, -1, slots & (LANES - 1)), LANES))
            pair_row = hot(lax.shift_right_arithmetic(slots, lane_bits), rows)
        values = as_rows(pick(applied, pair_lane, pair_row))
        found[0] += values[:lines]
        found[1] += values[lines:]
        for i in range(3):
            found[2 + i].append(message[base + i * lines : base + (i + 1) * lines])
    heads = [old] + [jnp.sum(total, axis=0, keepdims=True) for total in totals]
    heads.append(jnp.zeros((TOTALS - len(heads), LANES), jnp.float32))
    out_ref[:TOTALS] = jnp.concatenate(heads, axis=0)
    base, step = TOTALS, count * lines
    for i in range(5):
        out_ref[base + i * step : base + (i + 1) * step] = jnp.concatenate(found[i], axis=0)


def final_kernel(
    dom_axis,
    inner_axis,
    ordered,
    count,
    lines,
    *refs,
):
    messages = [ref[...] for ref in refs[:count]]
    (
        own_ref,
        pair_lane_ref,
        pair_row_ref,
        vector_ref,
        new_solution_ref,
        new_residual_ref,
        new_direction_ref,
    ) = refs[count:]
    rows = own_ref.shape[0]
    me = lax.axis_index(dom_axis)
    if not ordered:
        own, direct, far, relayed = messages
        far, relayed = (other_order(value, TOTALS, lines) for value in (far, relayed))
        even = lax.axis_index(inner_axis) == 0
        line = [own] + [None] * 3
        line[SPLIT[0]] = jnp.where(even, direct, relayed)
        line[SPLIT[1]] = jnp.where(even, relayed, direct)
        line[BOTH] = far
        low = (me & 1) == 0
        high = (me & 2) == 0
        line = [jnp.where(low, line[i], line[i ^ 1]) for i in range(4)]
        messages = [jnp.where(high, line[i], line[i ^ 2]) for i in range(4)]
    base = TOTALS
    step = (messages[0].shape[0] - base) // 5
    totals = messages[0][:base]
    for message in messages[1:]:
        totals = totals + message[:base]
    terms = [jnp.zeros((step, LANES), jnp.float32) for _ in range(3)]

    def part(message, i):
        return message[base + i * step : base + (i + 1) * step]

    from_left = jnp.zeros((lines, LANES), jnp.float32)
    from_right = jnp.zeros((lines, LANES), jnp.float32)
    for d in range(count - 1):
        near, next_one = messages[d], messages[d + 1]
        forward, backward = part(near, 0), part(next_one, 1)
        terms[0] += part(near, 2) * backward
        terms[1] += part(near, 3) * backward
        terms[2] += part(near, 4) * backward * (2.0 * forward + backward)
        from_left = jnp.where(me == d + 1, forward[:lines], from_left)
        from_right = jnp.where(me == d, backward[:lines], from_right)
    incoming = as_row(jnp.concatenate([from_right, from_left], axis=0))
    applied = own_ref[...] + place(incoming, pair_lane_ref[...], pair_row_ref[...])

    def whole(value):
        return jnp.sum(value, axis=1, keepdims=True)

    old = totals[0:1]
    curve, cross, square = (
        totals[i + 1 : i + 2] + jnp.sum(terms[i], axis=0, keepdims=True) for i in range(3)
    )
    old_norm = whole(old)
    step_size = old_norm / whole(curve)
    new_norm = whole(old - step_size * (2.0 * cross - step_size * square))
    solution, residual, direction, diagonal = (
        vector_ref[i * rows : (i + 1) * rows] for i in range(4)
    )
    new_residual = residual - step_size * applied
    new_solution_ref[...] = solution + step_size * direction
    new_residual_ref[...] = new_residual
    new_direction_ref[...] = diagonal * new_residual + (new_norm / old_norm) * direction


def other_order(message, base, lines):
    blocks = [message[:base]]
    for start in range(base, message.shape[0], 2 * lines):
        blocks += [message[start + lines : start + 2 * lines], message[start : start + lines]]
    return jnp.concatenate(blocks, axis=0)


def specs(spaces):
    return [pl.BlockSpec(memory_space=space) for space in spaces]


def swap_first(count):
    return [(i, i ^ 1) for i in range(count)]


def swap_second(count):
    return [(i, (i + 1 if i % 2 else i - 1) % count) for i in range(count)]


def local(
    solution,
    residual,
    direction,
    inverse_diagonal,
    schur_blocks,
    elem_dofs,
    element_order,
    left_slots,
    right_slots,
    share_count,
):
    group, dom = ("batch", "sub"), "dom"
    group_count, dom_count = lax.axis_size(group), lax.axis_size(dom)
    sub_count = lax.axis_size("sub")
    elements, size = elem_dofs.shape
    width = -(-size // LANES) * LANES
    pairs = left_slots.shape[1]
    lines = pairs // LANES
    rows = residual.shape[0] // LANES
    f32, bf16 = jnp.float32, jnp.bfloat16
    vmem = pltpu.VMEM
    params = pltpu.CompilerParams(vmem_limit_bytes=VMEM_LIMIT)

    solution, residual, direction, inverse_diagonal = (
        value.reshape(rows, LANES) for value in (solution, residual, direction, inverse_diagonal)
    )
    first = lax.ppermute(direction, group, swap_first(group_count))
    second = lax.ppermute(direction, group, swap_second(group_count))

    lane_hot, row_hot, pair_lane, pair_row, static, vectors = pl.pallas_call(
        functools.partial(prepare_kernel, group),
        out_shape=[
            jax.ShapeDtypeStruct((LANES, elements * width), bf16),
            jax.ShapeDtypeStruct((3 * rows, elements * width), f32),
            jax.ShapeDtypeStruct((LANES, 2 * pairs), bf16),
            jax.ShapeDtypeStruct((rows, 2 * pairs), f32),
            jax.ShapeDtypeStruct((STATIC, LANES), f32),
            jax.ShapeDtypeStruct((4 * rows, LANES), f32),
        ],
        in_specs=specs([pltpu.HBM] * 9),
        out_specs=specs([vmem] * 6),
        scratch_shapes=[
            pltpu.VMEM((elements, size), jnp.int32),
            pltpu.VMEM((8, width), jnp.int32),
            pltpu.VMEM((1, pairs), jnp.int32),
            pltpu.VMEM((1, pairs), jnp.int32),
            pltpu.SMEM((elements,), jnp.int32),
            pltpu.SMEM((1, 2), jnp.int32),
            pltpu.SemaphoreType.DMA((9,)),
        ],
        compiler_params=params,
        cost_estimate=pl.CostEstimate(flops=1600000000, bytes_accessed=16000000, transcendentals=0),
        name="prepare",
    )(
        *(
            pltpu.with_memory_space_constraint(value, pltpu.HBM)
            for value in (
                element_order,
                share_count,
                elem_dofs,
                left_slots,
                right_slots,
                solution,
                residual,
                direction,
                inverse_diagonal,
            )
        )
    )

    message = pl.pallas_call(
        element_kernel,
        out_shape=jax.ShapeDtypeStruct((SUMS + STATIC, LANES), f32),
        in_specs=specs([vmem] * 7),
        out_specs=pl.BlockSpec(memory_space=vmem),
        scratch_shapes=[pltpu.VMEM((8, width), f32), pltpu.VMEM((8, width), f32)],
        compiler_params=params,
        name="elements",
    )(vectors, first, second, schur_blocks, lane_hot, row_hot, static)

    if group_count == 4:
        first = lax.ppermute(message, group, swap_first(group_count))
        second = lax.ppermute(message, group, swap_second(group_count))
        relayed = lax.ppermute(second, group, swap_first(group_count))
        messages = [message, first, relayed, second]
    else:
        me = lax.axis_index(group)
        order = me ^ jnp.arange(group_count)
        everyone = lax.all_gather(message, group)
        second_of = jnp.array([target for _, target in swap_second(group_count)])
        moved = everyone[second_of[me ^ 3 ^ jnp.arange(group_count)], 2 * rows : 3 * rows]
        everyone = everyone[order].at[:, 2 * rows : 3 * rows].set(moved)
        messages = [everyone[m] for m in range(group_count)]

    own, message = pl.pallas_call(
        functools.partial(sum_kernel, group_count),
        out_shape=[
            jax.ShapeDtypeStruct((rows, LANES), f32),
            jax.ShapeDtypeStruct((TOTALS + 5 * group_count * lines, LANES), f32),
        ],
        in_specs=specs([vmem] * (group_count + 2)),
        out_specs=specs([vmem] * 2),
        compiler_params=params,
        name="sums",
    )(*messages, pair_lane, pair_row)

    ordered = not (dom_count == 4 and sub_count == 2)
    if ordered:
        everyone = lax.all_gather(message, dom)
        messages = [everyone[d] for d in range(dom_count)]
    else:
        line = (dom, "sub")
        split = [(2 * d + s, 2 * (d ^ SPLIT[s]) + s) for d in range(4) for s in range(2)]
        both = [(2 * d + s, 2 * (d ^ BOTH) + 1 - s) for d in range(4) for s in range(2)]
        direct = lax.ppermute(message, line, split)
        far = lax.ppermute(message, line, both)
        relayed = lax.ppermute(direct, "sub", [(0, 1), (1, 0)])
        messages = [message, direct, far, relayed]

    outputs = pl.pallas_call(
        functools.partial(final_kernel, dom, "sub", ordered, dom_count, lines),
        out_shape=[jax.ShapeDtypeStruct((rows, LANES), f32)] * 3,
        in_specs=specs([vmem] * (dom_count + 4)),
        out_specs=specs([vmem] * 3),
        compiler_params=params,
        name="update",
    )(*messages, own, pair_lane, pair_row, vectors)
    return tuple(value.reshape(-1) for value in outputs)


def solution(mesh):
    whole = P(("groups", "dom", "batch", "sub"))
    lines = P(("groups", "dom", "batch", "sub"), None)
    return jax.shard_map(
        local,
        mesh=mesh,
        in_specs=(whole,) * 4
        + (P(("groups", "dom", "batch", "sub"), None, None), lines, whole, lines, lines, lines),
        out_specs=(whole,) * 3,
        check_vma=False,
    )
```

```python
import functools

import jax
import jax.numpy as jnp
from jax import lax
from jax.experimental import pallas as pl
from jax.experimental.pallas import tpu as pltpu
from jax.sharding import PartitionSpec as P

ORDER = 10
LANES = 128
VMEM_LIMIT = 32 * 1024 * 1024
SUMS = 24
STATIC = 40
SPLIT, BOTH = (2, 3), 1
TOTALS = 8


def split(value):
    high = value.astype(jnp.bfloat16).astype(jnp.float32)
    rest = value - high
    middle = rest.astype(jnp.bfloat16).astype(jnp.float32)
    return [high, middle, rest - middle]


def half(value):
    return value.astype(jnp.bfloat16)


def look_up(table, low, high):
    found = jnp.zeros(low.shape, jnp.float32)
    for row in range(table.shape[0]):
        line = jnp.broadcast_to(table[row : row + 1], low.shape)
        line = jnp.take_along_axis(line, low, axis=1, mode="promise_in_bounds")
        found = jnp.where(high == row, line, found)
    return found


def lanes_of(slots):
    return slots & (LANES - 1), lax.shift_right_arithmetic(slots, LANES.bit_length() - 1)


def place(values, lane_hot, row_hot):
    rows = row_hot.shape[0]
    spread = jnp.concatenate([row_hot * part for part in split(values)], axis=0)
    parts = lax.dot_general(
        half(spread), lane_hot, (((1,), (1,)), ((), ())), preferred_element_type=jnp.float32
    )
    return (parts[:rows] + parts[rows : 2 * rows]) + parts[2 * rows :]


def hot(index, count):
    rows = lax.broadcasted_iota(jnp.int32, (count, index.shape[1]), 0)
    return jnp.where(rows == index, 1.0, 0.0)


def as_rows(row):
    return [row[:, i * LANES : (i + 1) * LANES] for i in range(row.shape[1] // LANES)]


def prepare_kernel(
    group_axes,
    order_hbm,
    count_hbm,
    dofs_hbm,
    left_hbm,
    right_hbm,
    solution_hbm,
    residual_hbm,
    direction_hbm,
    diagonal_hbm,
    lane_ref,
    row_ref,
    index_ref,
    static_ref,
    vector_ref,
    dofs_ref,
    wide_ref,
    left_ref,
    right_ref,
    order_ref,
    count_ref,
    sems,
):
    rows = direction_hbm.shape[0]
    moves = [
        (order_hbm, order_ref),
        (count_hbm, count_ref),
        (dofs_hbm, dofs_ref),
        (left_hbm, left_ref),
        (right_hbm, right_ref),
    ]
    for i, vector in enumerate((solution_hbm, residual_hbm, direction_hbm, diagonal_hbm)):
        moves.append((vector, vector_ref.at[i * rows : (i + 1) * rows]))
    copies = [pltpu.make_async_copy(*move, sems.at[i]) for i, move in enumerate(moves)]
    for copy in copies:
        copy.start()
    (outer, inner) = group_axes
    me = lax.axis_index(outer) * lax.axis_size(inner) + lax.axis_index(inner)
    elements, size = dofs_ref.shape
    width = wide_ref.shape[1]
    slot_bits = (rows * LANES - 1).bit_length()
    wide_ref[...] = jnp.zeros(wide_ref.shape, jnp.int32)
    lanes = lax.broadcasted_iota(jnp.int32, (1, width), 1)
    eighth = lax.broadcasted_iota(jnp.int32, (8, width), 0) == (
        lax.broadcasted_iota(jnp.int32, (8, width), 1) & 7
    )
    tile = jnp.where(
        lax.shift_right_logical(lax.broadcasted_iota(jnp.int32, (width, LANES), 0), 3)
        == lax.broadcasted_iota(jnp.int32, (width, LANES), 1),
        1.0,
        0.0,
    )
    for copy in copies:
        copy.wait()
    wide_ref[:elements, :size] = dofs_ref[...]
    parts = []
    for e in range(elements):
        order = order_ref[e]
        live = size * (6 * order * order + 2) // (6 * ORDER * ORDER + 2)
        active = lanes < live
        dofs = wide_ref[e : e + 1, :]
        piece = lax.shift_right_logical(dofs, slot_bits)
        place_of = jnp.where(piece == me, 0, jnp.where(piece == (me ^ 1), 1, 2))
        low, high = lanes_of(dofs)
        high = place_of * rows + (high & (rows - 1))
        low = jnp.where(active, low, -1)
        high = jnp.where(active, high, -1)
        lane_ref[:, e * width : (e + 1) * width] = half(hot(low, LANES))
        row_ref[:, e * width : (e + 1) * width] = hot(high, 3 * rows)
        for value in (low, high):
            parts.append(jnp.where(eighth, (value + 1).astype(jnp.float32), 0.0))
    packed = jnp.dot(
        half(jnp.concatenate(parts, axis=0)), half(tile), preferred_element_type=jnp.float32
    )
    packed = packed.astype(jnp.int32) - 1
    for e in range(elements):
        index_ref[16 * e : 16 * e + 8] = jnp.maximum(packed[16 * e : 16 * e + 8], 0)
        index_ref[16 * e + 8 : 16 * e + 16] = packed[16 * e + 8 : 16 * e + 16]
    pairs = left_ref.shape[1]
    pair_lanes = lax.broadcasted_iota(jnp.int32, (1, pairs), 1)
    right = jnp.where(pair_lanes < count_ref[0, 1], right_ref[...], -1)
    left = jnp.where(pair_lanes < count_ref[0, 0], left_ref[...], -1)
    slots = jnp.concatenate([right, left], axis=1)
    low, high = lanes_of(slots)
    position = lax.broadcasted_iota(jnp.int32, slots.shape, 1)
    source = place(
        (position + 1).astype(jnp.float32),
        half(hot(jnp.where(slots < 0, -1, low), LANES)),
        hot(high, rows),
    )
    source = source.astype(jnp.int32) - 1
    low, high = lanes_of(source)
    index_ref[16 * elements : 16 * elements + 8] = low
    index_ref[16 * elements + 8 : 16 * elements + 16] = high
    owner = jnp.where(source >= pairs, 0.0, 1.0)
    residual = vector_ref[rows : 2 * rows]
    direction = vector_ref[2 * rows : 3 * rows]
    diagonal = vector_ref[3 * rows : 4 * rows]
    scaled = diagonal * residual
    static_ref[0:8] = owner * diagonal
    static_ref[8:16] = owner * direction
    static_ref[16:24] = owner * scaled
    lists = as_rows(slots)
    count = len(lists)
    lists = jnp.concatenate(lists + [jnp.full((8 - count, LANES), -1, jnp.int32)], axis=0)
    lines = [lists[:count].astype(jnp.float32)]
    lines.append(jnp.sum(owner * scaled * residual, axis=0, keepdims=True))
    for table in (direction, scaled, diagonal):
        lines.append(look_up(table, *lanes_of(lists))[: count // 2])
    used = 24 + count + 1 + 3 * (count // 2)
    lines.append(jnp.zeros((STATIC - used, LANES), jnp.float32))
    static_ref[24:STATIC] = jnp.concatenate(lines, axis=0)


def element_kernel(
    vector_ref, first_ref, second_ref, blocks_ref, lane_ref, row_ref, index_ref, static_ref, out_ref
):
    elements, size, _ = blocks_ref.shape
    width = lane_ref.shape[1] // elements
    rows = first_ref.shape[0]
    window = jnp.concatenate(
        [vector_ref[2 * rows : 3 * rows], first_ref[...], second_ref[...]], axis=0
    )
    whole = size // 8 * 8
    sums = None
    for e in range(elements):
        low, high = index_ref[16 * e : 16 * e + 8], index_ref[16 * e + 8 : 16 * e + 16]
        element_in = look_up(window, low, high)
        total = jnp.zeros((8, size), jnp.float32)
        for i in range(size // 8):
            total += blocks_ref[e, 8 * i : 8 * i + 8, :] * element_in[:, i : i + 1]
        total = jnp.sum(total, axis=0, keepdims=True)
        for i in range(size % 8):
            value = element_in[i : i + 1, size // 8 : size // 8 + 1]
            total += blocks_ref[e, whole + i : whole + i + 1, :] * value
        row_hot = row_ref[:, e * width : e * width + size]
        spread = half(jnp.concatenate([row_hot * part for part in split(total)], axis=0))
        part = lax.dot_general(
            spread,
            lane_ref[:, e * width : e * width + size],
            (((1,), (1,)), ((), ())),
            preferred_element_type=jnp.float32,
        )
        sums = part if sums is None else sums + part
    out_ref[:SUMS] = (sums[:SUMS] + sums[SUMS : 2 * SUMS]) + sums[2 * SUMS :]
    out_ref[SUMS:] = static_ref[...]


def sum_kernel(count, *refs):
    messages, (own_ref, out_ref) = refs[:count], refs[count:]
    rows = own_ref.shape[0]
    lines = (out_ref.shape[0] - TOTALS) // (5 * count)
    totals = [jnp.zeros((rows, LANES), jnp.float32) for _ in range(3)]
    old = jnp.zeros((1, LANES), jnp.float32)
    found = [[] for _ in range(5)]
    for m, message in enumerate(messages):
        applied = message[0:8] + messages[m ^ 1][8:16] + messages[m ^ 3][16:24]
        at = functools.partial(lambda ref, i: ref[SUMS + 8 * i : SUMS + 8 * i + 8], message)
        totals[0] += at(1) * applied
        totals[1] += at(2) * applied
        totals[2] += at(0) * applied * applied
        base = SUMS + 24
        if m == 0:
            own_ref[...] = applied
        low, high = lanes_of(message[base : base + 8].astype(jnp.int32))
        values = look_up(applied, low, high)
        found[0].append(values[:lines])
        found[1].append(values[lines : 2 * lines])
        base += 2 * lines
        old += message[base : base + 1]
        base += 1
        for i in range(3):
            found[2 + i].append(message[base + i * lines : base + (i + 1) * lines])
    heads = [old] + [jnp.sum(total, axis=0, keepdims=True) for total in totals]
    heads.append(jnp.zeros((TOTALS - len(heads), LANES), jnp.float32))
    out_ref[:TOTALS] = jnp.concatenate(heads, axis=0)
    base, step = TOTALS, count * lines
    for i in range(5):
        out_ref[base + i * step : base + (i + 1) * step] = jnp.concatenate(found[i], axis=0)


def final_kernel(
    dom_axis,
    inner_axis,
    ordered,
    count,
    lines,
    *refs,
):
    messages = [ref[...] for ref in refs[:count]]
    (
        own_ref,
        index_ref,
        vector_ref,
        new_solution_ref,
        new_residual_ref,
        new_direction_ref,
    ) = refs[count:]
    rows = own_ref.shape[0]
    me = lax.axis_index(dom_axis)
    if not ordered:
        own, direct, far, relayed = messages
        far, relayed = (other_order(value, TOTALS, lines) for value in (far, relayed))
        even = lax.axis_index(inner_axis) == 0
        line = [own] + [None] * 3
        line[SPLIT[0]] = jnp.where(even, direct, relayed)
        line[SPLIT[1]] = jnp.where(even, relayed, direct)
        line[BOTH] = far
        low = (me & 1) == 0
        high = (me & 2) == 0
        line = [jnp.where(low, line[i], line[i ^ 1]) for i in range(4)]
        messages = [jnp.where(high, line[i], line[i ^ 2]) for i in range(4)]
    base = TOTALS
    step = (messages[0].shape[0] - base) // 5
    totals = messages[0][:base]
    for message in messages[1:]:
        totals = totals + message[:base]
    terms = [jnp.zeros((step, LANES), jnp.float32) for _ in range(3)]

    def part(message, i):
        return message[base + i * step : base + (i + 1) * step]

    from_left = jnp.zeros((lines, LANES), jnp.float32)
    from_right = jnp.zeros((lines, LANES), jnp.float32)
    for d in range(count - 1):
        near, next_one = messages[d], messages[d + 1]
        forward, backward = part(near, 0), part(next_one, 1)
        terms[0] += part(near, 2) * backward
        terms[1] += part(near, 3) * backward
        terms[2] += part(near, 4) * backward * (2.0 * forward + backward)
        from_left = jnp.where(me == d + 1, forward[:lines], from_left)
        from_right = jnp.where(me == d, backward[:lines], from_right)
    incoming = jnp.concatenate([from_right, from_left], axis=0)
    last = index_ref.shape[0]
    applied = own_ref[...] + look_up(
        incoming, index_ref[last - 16 : last - 8], index_ref[last - 8 : last]
    )

    def whole(value):
        return jnp.sum(value, axis=1, keepdims=True)

    old = totals[0:1]
    curve, cross, square = (
        totals[i + 1 : i + 2] + jnp.sum(terms[i], axis=0, keepdims=True) for i in range(3)
    )
    old_norm = whole(old)
    step_size = old_norm / whole(curve)
    new_norm = whole(old - step_size * (2.0 * cross - step_size * square))
    solution, residual, direction, diagonal = (
        vector_ref[i * rows : (i + 1) * rows] for i in range(4)
    )
    new_residual = residual - step_size * applied
    new_solution_ref[...] = solution + step_size * direction
    new_residual_ref[...] = new_residual
    new_direction_ref[...] = diagonal * new_residual + (new_norm / old_norm) * direction


def other_order(message, base, lines):
    blocks = [message[:base]]
    for start in range(base, message.shape[0], 2 * lines):
        blocks += [message[start + lines : start + 2 * lines], message[start : start + lines]]
    return jnp.concatenate(blocks, axis=0)


def specs(spaces):
    return [pl.BlockSpec(memory_space=space) for space in spaces]


def swap_first(count):
    return [(i, i ^ 1) for i in range(count)]


def swap_second(count):
    return [(i, (i + 1 if i % 2 else i - 1) % count) for i in range(count)]


def local(
    solution,
    residual,
    direction,
    inverse_diagonal,
    schur_blocks,
    elem_dofs,
    element_order,
    left_slots,
    right_slots,
    share_count,
):
    group, dom = ("batch", "sub"), "dom"
    group_count, dom_count = lax.axis_size(group), lax.axis_size(dom)
    sub_count = lax.axis_size("sub")
    elements, size = elem_dofs.shape
    width = -(-size // LANES) * LANES
    pairs = left_slots.shape[1]
    lines = pairs // LANES
    rows = residual.shape[0] // LANES
    f32, bf16 = jnp.float32, jnp.bfloat16
    vmem = pltpu.VMEM
    params = pltpu.CompilerParams(vmem_limit_bytes=VMEM_LIMIT)

    solution, residual, direction, inverse_diagonal = (
        value.reshape(rows, LANES) for value in (solution, residual, direction, inverse_diagonal)
    )
    first = lax.ppermute(direction, group, swap_first(group_count))
    second = lax.ppermute(direction, group, swap_second(group_count))

    lane_hot, row_hot, index, static, vectors = pl.pallas_call(
        functools.partial(prepare_kernel, group),
        out_shape=[
            jax.ShapeDtypeStruct((LANES, elements * width), bf16),
            jax.ShapeDtypeStruct((3 * rows, elements * width), f32),
            jax.ShapeDtypeStruct((16 * (elements + 1), LANES), jnp.int32),
            jax.ShapeDtypeStruct((STATIC, LANES), f32),
            jax.ShapeDtypeStruct((4 * rows, LANES), f32),
        ],
        in_specs=specs([pltpu.HBM] * 9),
        out_specs=specs([vmem] * 5),
        scratch_shapes=[
            pltpu.VMEM((elements, size), jnp.int32),
            pltpu.VMEM((8, width), jnp.int32),
            pltpu.VMEM((1, pairs), jnp.int32),
            pltpu.VMEM((1, pairs), jnp.int32),
            pltpu.SMEM((elements,), jnp.int32),
            pltpu.SMEM((1, 2), jnp.int32),
            pltpu.SemaphoreType.DMA((9,)),
        ],
        compiler_params=params,
        cost_estimate=pl.CostEstimate(flops=1600000000, bytes_accessed=16000000, transcendentals=0),
        name="prepare",
    )(
        *(
            pltpu.with_memory_space_constraint(value, pltpu.HBM)
            for value in (
                element_order,
                share_count,
                elem_dofs,
                left_slots,
                right_slots,
                solution,
                residual,
                direction,
                inverse_diagonal,
            )
        )
    )

    message = pl.pallas_call(
        element_kernel,
        out_shape=jax.ShapeDtypeStruct((SUMS + STATIC, LANES), f32),
        in_specs=specs([vmem] * 8),
        out_specs=pl.BlockSpec(memory_space=vmem),
        compiler_params=params,
        name="elements",
    )(vectors, first, second, schur_blocks, lane_hot, row_hot, index, static)

    if group_count == 4:
        first = lax.ppermute(message, group, swap_first(group_count))
        second = lax.ppermute(message, group, swap_second(group_count))
        relayed = lax.ppermute(second, group, swap_first(group_count))
        messages = [message, first, relayed, second]
    else:
        me = lax.axis_index(group)
        order = me ^ jnp.arange(group_count)
        everyone = lax.all_gather(message, group)
        second_of = jnp.array([target for _, target in swap_second(group_count)])
        moved = everyone[second_of[me ^ 3 ^ jnp.arange(group_count)], 2 * rows : 3 * rows]
        everyone = everyone[order].at[:, 2 * rows : 3 * rows].set(moved)
        messages = [everyone[m] for m in range(group_count)]

    own, message = pl.pallas_call(
        functools.partial(sum_kernel, group_count),
        out_shape=[
            jax.ShapeDtypeStruct((rows, LANES), f32),
            jax.ShapeDtypeStruct((TOTALS + 5 * group_count * lines, LANES), f32),
        ],
        in_specs=specs([vmem] * group_count),
        out_specs=specs([vmem] * 2),
        compiler_params=params,
        name="sums",
    )(*messages)

    ordered = not (dom_count == 4 and sub_count == 2)
    if ordered:
        everyone = lax.all_gather(message, dom)
        messages = [everyone[d] for d in range(dom_count)]
    else:
        line = (dom, "sub")
        split = [(2 * d + s, 2 * (d ^ SPLIT[s]) + s) for d in range(4) for s in range(2)]
        both = [(2 * d + s, 2 * (d ^ BOTH) + 1 - s) for d in range(4) for s in range(2)]
        direct = lax.ppermute(message, line, split)
        far = lax.ppermute(message, line, both)
        relayed = lax.ppermute(direct, "sub", [(0, 1), (1, 0)])
        messages = [message, direct, far, relayed]

    outputs = pl.pallas_call(
        functools.partial(final_kernel, dom, "sub", ordered, dom_count, lines),
        out_shape=[jax.ShapeDtypeStruct((rows, LANES), f32)] * 3,
        in_specs=specs([vmem] * (dom_count + 3)),
        out_specs=specs([vmem] * 3),
        compiler_params=params,
        name="update",
    )(*messages, own, index, vectors)
    return tuple(value.reshape(-1) for value in outputs)


def solution(mesh):
    whole = P(("groups", "dom", "batch", "sub"))
    lines = P(("groups", "dom", "batch", "sub"), None)
    return jax.shard_map(
        local,
        mesh=mesh,
        in_specs=(whole,) * 4
        + (P(("groups", "dom", "batch", "sub"), None, None), lines, whole, lines, lines, lines),
        out_specs=(whole,) * 3,
        check_vma=False,
    )
```

```python
import functools

import jax
import jax.numpy as jnp
from jax import lax
from jax.experimental import pallas as pl
from jax.experimental.pallas import tpu as pltpu
from jax.sharding import PartitionSpec as P

ORDER = 10
LANES = 128
VMEM_LIMIT = 32 * 1024 * 1024
SUMS = 24
STATIC = 40
SPLIT, BOTH = (2, 3), 1
TOTALS = 8


def split(value):
    high = value.astype(jnp.bfloat16).astype(jnp.float32)
    rest = value - high
    middle = rest.astype(jnp.bfloat16).astype(jnp.float32)
    return [high, middle, rest - middle]


def half(value):
    return value.astype(jnp.bfloat16)


def look_up(table, low, high, found=None):
    if found is None:
        found = jnp.zeros(low.shape, jnp.float32)
    for row in range(table.shape[0]):
        line = jnp.broadcast_to(table[row : row + 1], low.shape)
        line = jnp.take_along_axis(line, low, axis=1, mode="promise_in_bounds")
        found = jnp.where(high == row, line, found)
    return found


def spread_lane(value, lane):
    index = jnp.full(value.shape, lane, jnp.int32)
    return jnp.take_along_axis(value, index, axis=1, mode="promise_in_bounds")


def lanes_of(slots):
    return slots & (LANES - 1), lax.shift_right_arithmetic(slots, LANES.bit_length() - 1)


def place(values, lane_hot, row_hot):
    rows = row_hot.shape[0]
    spread = jnp.concatenate([row_hot * part for part in split(values)], axis=0)
    parts = lax.dot_general(
        half(spread), lane_hot, (((1,), (1,)), ((), ())), preferred_element_type=jnp.float32
    )
    return (parts[:rows] + parts[rows : 2 * rows]) + parts[2 * rows :]


def hot(index, count):
    rows = lax.broadcasted_iota(jnp.int32, (count, index.shape[1]), 0)
    return jnp.where(rows == index, 1.0, 0.0)


def as_rows(row):
    return [row[:, i * LANES : (i + 1) * LANES] for i in range(row.shape[1] // LANES)]


def prepare_kernel(
    group_axes,
    order_hbm,
    count_hbm,
    dofs_hbm,
    left_hbm,
    right_hbm,
    solution_hbm,
    residual_hbm,
    direction_hbm,
    diagonal_hbm,
    lane_ref,
    row_ref,
    index_ref,
    in_ref,
    static_ref,
    vector_ref,
    dofs_ref,
    wide_ref,
    left_ref,
    right_ref,
    order_ref,
    count_ref,
    sems,
):
    rows = direction_hbm.shape[0]
    moves = [
        (order_hbm, order_ref),
        (count_hbm, count_ref),
        (dofs_hbm, dofs_ref),
        (left_hbm, left_ref),
        (right_hbm, right_ref),
    ]
    for i, vector in enumerate((solution_hbm, residual_hbm, direction_hbm, diagonal_hbm)):
        moves.append((vector, vector_ref.at[i * rows : (i + 1) * rows]))
    copies = [pltpu.make_async_copy(*move, sems.at[i]) for i, move in enumerate(moves)]
    for copy in copies:
        copy.start()
    (outer, inner) = group_axes
    me = lax.axis_index(outer) * lax.axis_size(inner) + lax.axis_index(inner)
    elements, size = dofs_ref.shape
    width = wide_ref.shape[1]
    slot_bits = (rows * LANES - 1).bit_length()
    wide_ref[...] = jnp.zeros(wide_ref.shape, jnp.int32)
    lanes = lax.broadcasted_iota(jnp.int32, (1, width), 1)
    eighth = lax.broadcasted_iota(jnp.int32, (8, width), 0) == (
        lax.broadcasted_iota(jnp.int32, (8, width), 1) & 7
    )
    tile = jnp.where(
        lax.shift_right_logical(lax.broadcasted_iota(jnp.int32, (width, LANES), 0), 3)
        == lax.broadcasted_iota(jnp.int32, (width, LANES), 1),
        1.0,
        0.0,
    )
    for copy in copies:
        copy.wait()
    wide_ref[:elements, :size] = dofs_ref[...]
    parts = []
    for e in range(elements):
        order = order_ref[e]
        live = size * (6 * order * order + 2) // (6 * ORDER * ORDER + 2)
        active = lanes < live
        dofs = wide_ref[e : e + 1, :]
        piece = lax.shift_right_logical(dofs, slot_bits)
        place_of = jnp.where(piece == me, 0, jnp.where(piece == (me ^ 1), 1, 2))
        low, high = lanes_of(dofs)
        high = place_of * rows + (high & (rows - 1))
        low = jnp.where(active, low, -1)
        high = jnp.where(active, high, -1)
        lane_ref[:, e * width : (e + 1) * width] = half(hot(low, LANES))
        row_ref[:, e * width : (e + 1) * width] = hot(high, 3 * rows)
        for value in (low, high):
            parts.append(jnp.where(eighth, (value + 1).astype(jnp.float32), 0.0))
    packed = jnp.dot(
        half(jnp.concatenate(parts, axis=0)), half(tile), preferred_element_type=jnp.float32
    )
    tiles = -(-size // 8)
    packed = [packed[16 * e : 16 * e + 16, :tiles] for e in range(elements)]
    registers = in_ref.shape[0] // 8
    packed.append(jnp.zeros((16, registers * LANES - elements * tiles), jnp.float32))
    packed = jnp.concatenate(packed, axis=1).astype(jnp.int32) - 1
    direction = vector_ref[2 * rows : 3 * rows]
    for i in range(registers):
        register = packed[:, i * LANES : (i + 1) * LANES]
        low, high = jnp.maximum(register[:8], 0), register[8:]
        index_ref[16 * i : 16 * i + 8] = low
        index_ref[16 * i + 8 : 16 * i + 16] = high - rows
        in_ref[8 * i : 8 * i + 8] = look_up(direction, low, high)
    pairs = left_ref.shape[1]
    pair_lanes = lax.broadcasted_iota(jnp.int32, (1, pairs), 1)
    right = jnp.where(pair_lanes < count_ref[0, 1], right_ref[...], -1)
    left = jnp.where(pair_lanes < count_ref[0, 0], left_ref[...], -1)
    slots = jnp.concatenate([right, left], axis=1)
    low, high = lanes_of(slots)
    position = lax.broadcasted_iota(jnp.int32, slots.shape, 1)
    source = place(
        (position + 1).astype(jnp.float32),
        half(hot(jnp.where(slots < 0, -1, low), LANES)),
        hot(high, rows),
    )
    source = source.astype(jnp.int32) - 1
    low, high = lanes_of(source)
    index_ref[16 * registers : 16 * registers + 8] = low
    index_ref[16 * registers + 8 : 16 * registers + 16] = high
    owner = jnp.where(source >= pairs, 0.0, 1.0)
    residual = vector_ref[rows : 2 * rows]
    diagonal = vector_ref[3 * rows : 4 * rows]
    scaled = diagonal * residual
    static_ref[0:8] = owner * diagonal
    static_ref[8:16] = owner * direction
    static_ref[16:24] = owner * scaled
    lists = as_rows(slots)
    count = len(lists)
    lists = jnp.concatenate(lists + [jnp.full((8 - count, LANES), -1, jnp.int32)], axis=0)
    lines = [lists[:count].astype(jnp.float32)]
    lines.append(jnp.sum(owner * scaled * residual, axis=0, keepdims=True))
    for table in (direction, scaled, diagonal):
        lines.append(look_up(table, *lanes_of(lists))[: count // 2])
    used = 24 + count + 1 + 3 * (count // 2)
    lines.append(jnp.zeros((STATIC - used, LANES), jnp.float32))
    static_ref[24:STATIC] = jnp.concatenate(lines, axis=0)


def element_kernel(
    first_ref, second_ref, blocks_ref, lane_ref, row_ref, index_ref, in_ref, static_ref, out_ref
):
    elements, size, _ = blocks_ref.shape
    width = lane_ref.shape[1] // elements
    tiles = -(-size // 8)
    whole = size // 8 * 8
    window = jnp.concatenate([first_ref[...], second_ref[...]], axis=0)
    element_in = [
        look_up(
            window,
            index_ref[16 * i : 16 * i + 8],
            index_ref[16 * i + 8 : 16 * i + 16],
            in_ref[8 * i : 8 * i + 8],
        )
        for i in range(in_ref.shape[0] // 8)
    ]
    sums = None
    for e in range(elements):
        total = jnp.zeros((8, size), jnp.float32)
        for i in range(tiles):
            column = e * tiles + i
            value = spread_lane(element_in[column // LANES], column % LANES)
            value = jnp.concatenate([value] * (width // LANES), axis=1)[:, :size]
            if 8 * i < whole:
                total += blocks_ref[e, 8 * i : 8 * i + 8, :] * value
        total = jnp.sum(total, axis=0, keepdims=True)
        for i in range(size % 8):
            total += blocks_ref[e, whole + i : whole + i + 1, :] * value[i : i + 1]
        row_hot = row_ref[:, e * width : e * width + size]
        spread = half(jnp.concatenate([row_hot * part for part in split(total)], axis=0))
        part = lax.dot_general(
            spread,
            lane_ref[:, e * width : e * width + size],
            (((1,), (1,)), ((), ())),
            preferred_element_type=jnp.float32,
        )
        sums = part if sums is None else sums + part
    out_ref[:SUMS] = (sums[:SUMS] + sums[SUMS : 2 * SUMS]) + sums[2 * SUMS :]
    out_ref[SUMS:] = static_ref[...]


def sum_kernel(count, *refs):
    messages, (own_ref, out_ref) = refs[:count], refs[count:]
    rows = own_ref.shape[0]
    lines = (out_ref.shape[0] - TOTALS) // (5 * count)
    totals = [jnp.zeros((rows, LANES), jnp.float32) for _ in range(3)]
    old = jnp.zeros((1, LANES), jnp.float32)
    found = [[] for _ in range(5)]
    for m, message in enumerate(messages):
        applied = message[0:8] + messages[m ^ 1][8:16] + messages[m ^ 3][16:24]
        at = functools.partial(lambda ref, i: ref[SUMS + 8 * i : SUMS + 8 * i + 8], message)
        totals[0] += at(1) * applied
        totals[1] += at(2) * applied
        totals[2] += at(0) * applied * applied
        base = SUMS + 24
        if m == 0:
            own_ref[...] = applied
        low, high = lanes_of(message[base : base + 8].astype(jnp.int32))
        values = look_up(applied, low, high)
        found[0].append(values[:lines])
        found[1].append(values[lines : 2 * lines])
        base += 2 * lines
        old += message[base : base + 1]
        base += 1
        for i in range(3):
            found[2 + i].append(message[base + i * lines : base + (i + 1) * lines])
    heads = [old] + [jnp.sum(total, axis=0, keepdims=True) for total in totals]
    heads.append(jnp.zeros((TOTALS - len(heads), LANES), jnp.float32))
    out_ref[:TOTALS] = jnp.concatenate(heads, axis=0)
    base, step = TOTALS, count * lines
    for i in range(5):
        out_ref[base + i * step : base + (i + 1) * step] = jnp.concatenate(found[i], axis=0)


def final_kernel(
    dom_axis,
    inner_axis,
    ordered,
    count,
    lines,
    *refs,
):
    messages = [ref[...] for ref in refs[:count]]
    (
        own_ref,
        index_ref,
        vector_ref,
        new_solution_ref,
        new_residual_ref,
        new_direction_ref,
    ) = refs[count:]
    rows = own_ref.shape[0]
    me = lax.axis_index(dom_axis)
    if not ordered:
        own, direct, near, relayed = messages
        direct = other_order(direct, TOTALS, lines)
        even = lax.axis_index(inner_axis) == 0
        line = [own] + [None] * 3
        line[SPLIT[0]] = jnp.where(even, relayed, direct)
        line[SPLIT[1]] = jnp.where(even, direct, relayed)
        line[BOTH] = near
        low = (me & 1) == 0
        high = (me & 2) == 0
        line = [jnp.where(low, line[i], line[i ^ 1]) for i in range(4)]
        messages = [jnp.where(high, line[i], line[i ^ 2]) for i in range(4)]
    base = TOTALS
    step = (messages[0].shape[0] - base) // 5
    totals = messages[0][:base]
    for message in messages[1:]:
        totals = totals + message[:base]
    terms = [jnp.zeros((step, LANES), jnp.float32) for _ in range(3)]

    def part(message, i):
        return message[base + i * step : base + (i + 1) * step]

    from_left = jnp.zeros((lines, LANES), jnp.float32)
    from_right = jnp.zeros((lines, LANES), jnp.float32)
    for d in range(count - 1):
        near, next_one = messages[d], messages[d + 1]
        forward, backward = part(near, 0), part(next_one, 1)
        terms[0] += part(near, 2) * backward
        terms[1] += part(near, 3) * backward
        terms[2] += part(near, 4) * backward * (2.0 * forward + backward)
        from_left = jnp.where(me == d + 1, forward[:lines], from_left)
        from_right = jnp.where(me == d, backward[:lines], from_right)
    incoming = jnp.concatenate([from_right, from_left], axis=0)
    last = index_ref.shape[0]
    applied = own_ref[...] + look_up(
        incoming, index_ref[last - 16 : last - 8], index_ref[last - 8 : last]
    )

    def whole(value):
        return jnp.sum(value, axis=1, keepdims=True)

    old = totals[0:1]
    curve, cross, square = (
        totals[i + 1 : i + 2] + jnp.sum(terms[i], axis=0, keepdims=True) for i in range(3)
    )
    old_norm = whole(old)
    step_size = old_norm / whole(curve)
    new_norm = whole(old - step_size * (2.0 * cross - step_size * square))
    solution, residual, direction, diagonal = (
        vector_ref[i * rows : (i + 1) * rows] for i in range(4)
    )
    new_residual = residual - step_size * applied
    new_solution_ref[...] = solution + step_size * direction
    new_residual_ref[...] = new_residual
    new_direction_ref[...] = diagonal * new_residual + (new_norm / old_norm) * direction


def other_order(message, base, lines):
    blocks = [message[:base]]
    for start in range(base, message.shape[0], 2 * lines):
        blocks += [message[start + lines : start + 2 * lines], message[start : start + lines]]
    return jnp.concatenate(blocks, axis=0)


def specs(spaces):
    return [pl.BlockSpec(memory_space=space) for space in spaces]


def swap_first(count):
    return [(i, i ^ 1) for i in range(count)]


def swap_second(count):
    return [(i, (i + 1 if i % 2 else i - 1) % count) for i in range(count)]


def local(
    solution,
    residual,
    direction,
    inverse_diagonal,
    schur_blocks,
    elem_dofs,
    element_order,
    left_slots,
    right_slots,
    share_count,
):
    group, dom = ("batch", "sub"), "dom"
    group_count, dom_count = lax.axis_size(group), lax.axis_size(dom)
    sub_count = lax.axis_size("sub")
    elements, size = elem_dofs.shape
    width = -(-size // LANES) * LANES
    pairs = left_slots.shape[1]
    lines = pairs // LANES
    rows = residual.shape[0] // LANES
    f32, bf16 = jnp.float32, jnp.bfloat16
    vmem = pltpu.VMEM
    params = pltpu.CompilerParams(vmem_limit_bytes=VMEM_LIMIT)

    solution, residual, direction, inverse_diagonal = (
        value.reshape(rows, LANES) for value in (solution, residual, direction, inverse_diagonal)
    )
    first = lax.ppermute(direction, group, swap_first(group_count))
    second = lax.ppermute(direction, group, swap_second(group_count))

    registers = -(-elements * -(-size // 8) // LANES)
    lane_hot, row_hot, index, element_in, static, vectors = pl.pallas_call(
        functools.partial(prepare_kernel, group),
        out_shape=[
            jax.ShapeDtypeStruct((LANES, elements * width), bf16),
            jax.ShapeDtypeStruct((3 * rows, elements * width), f32),
            jax.ShapeDtypeStruct((16 * (registers + 1), LANES), jnp.int32),
            jax.ShapeDtypeStruct((8 * registers, LANES), f32),
            jax.ShapeDtypeStruct((STATIC, LANES), f32),
            jax.ShapeDtypeStruct((4 * rows, LANES), f32),
        ],
        in_specs=specs([pltpu.HBM] * 9),
        out_specs=specs([vmem] * 6),
        scratch_shapes=[
            pltpu.VMEM((elements, size), jnp.int32),
            pltpu.VMEM((8, width), jnp.int32),
            pltpu.VMEM((1, pairs), jnp.int32),
            pltpu.VMEM((1, pairs), jnp.int32),
            pltpu.SMEM((elements,), jnp.int32),
            pltpu.SMEM((1, 2), jnp.int32),
            pltpu.SemaphoreType.DMA((9,)),
        ],
        compiler_params=params,
        cost_estimate=pl.CostEstimate(flops=1600000000, bytes_accessed=16000000, transcendentals=0),
        name="prepare",
    )(
        *(
            pltpu.with_memory_space_constraint(value, pltpu.HBM)
            for value in (
                element_order,
                share_count,
                elem_dofs,
                left_slots,
                right_slots,
                solution,
                residual,
                direction,
                inverse_diagonal,
            )
        )
    )

    message = pl.pallas_call(
        element_kernel,
        out_shape=jax.ShapeDtypeStruct((SUMS + STATIC, LANES), f32),
        in_specs=specs([vmem] * 8),
        out_specs=pl.BlockSpec(memory_space=vmem),
        compiler_params=params,
        name="elements",
    )(first, second, schur_blocks, lane_hot, row_hot, index, element_in, static)

    if group_count == 4:
        first = lax.ppermute(message, group, swap_first(group_count))
        second = lax.ppermute(message, group, swap_second(group_count))
        relayed = lax.ppermute(second, group, swap_first(group_count))
        messages = [message, first, relayed, second]
    else:
        me = lax.axis_index(group)
        order = me ^ jnp.arange(group_count)
        everyone = lax.all_gather(message, group)
        second_of = jnp.array([target for _, target in swap_second(group_count)])
        moved = everyone[second_of[me ^ 3 ^ jnp.arange(group_count)], 2 * rows : 3 * rows]
        everyone = everyone[order].at[:, 2 * rows : 3 * rows].set(moved)
        messages = [everyone[m] for m in range(group_count)]

    own, message = pl.pallas_call(
        functools.partial(sum_kernel, group_count),
        out_shape=[
            jax.ShapeDtypeStruct((rows, LANES), f32),
            jax.ShapeDtypeStruct((TOTALS + 5 * group_count * lines, LANES), f32),
        ],
        in_specs=specs([vmem] * group_count),
        out_specs=specs([vmem] * 2),
        compiler_params=params,
        name="sums",
    )(*messages)

    ordered = not (dom_count == 4 and sub_count == 2)
    if ordered:
        everyone = lax.all_gather(message, dom)
        messages = [everyone[d] for d in range(dom_count)]
    else:
        line = (dom, "sub")
        split = [(2 * d + s, 2 * (d ^ SPLIT[s]) + 1 - s) for d in range(4) for s in range(2)]
        both = [(2 * d + s, 2 * (d ^ BOTH) + s) for d in range(4) for s in range(2)]
        direct = lax.ppermute(message, line, split)
        near = lax.ppermute(message, line, both)
        relayed = lax.ppermute(direct, "sub", [(0, 1), (1, 0)])
        messages = [message, direct, near, relayed]

    outputs = pl.pallas_call(
        functools.partial(final_kernel, dom, "sub", ordered, dom_count, lines),
        out_shape=[jax.ShapeDtypeStruct((rows, LANES), f32)] * 3,
        in_specs=specs([vmem] * (dom_count + 3)),
        out_specs=specs([vmem] * 3),
        compiler_params=params,
        name="update",
    )(*messages, own, index, vectors)
    return tuple(value.reshape(-1) for value in outputs)


def solution(mesh):
    whole = P(("groups", "dom", "batch", "sub"))
    lines = P(("groups", "dom", "batch", "sub"), None)
    return jax.shard_map(
        local,
        mesh=mesh,
        in_specs=(whole,) * 4
        + (P(("groups", "dom", "batch", "sub"), None, None), lines, whole, lines, lines, lines),
        out_specs=(whole,) * 3,
        check_vma=False,
    )
```
